128 devices in a mesh: section: 4 (over x), dp: 32 (over y, z, core).
Axes of the slice: x: 4, y: 4, z: 4, core: 2. Of those that a mesh axis runs over, the one named last changes fastest.
Arguments:
- gradient: bfloat16 [4, 32, 512, 512], P('section', None, 'dp'), may hold values from -6 to 6
- left_gram: float32 [4, 32, 512, 512], P('section', None, 'dp'), may hold values from -5 to 77, as said below
- right_gram: float32 [4, 32, 512, 512], P('section', None, 'dp'), may hold values from -5 to 77, as said below
- left_basis: float32 [4, 32, 512, 512], P('section', None, 'dp'), may hold values from -1 to 2
- right_basis: float32 [4, 32, 512, 512], P('section', None, 'dp'), may hold values from -1 to 2
- migration: int32 [4, 4], replicated, may hold values from 0 to 3, each once within a row
- owners: int32 [4, 32, 1], replicated, may hold values from 0 to 31; in each aligned block of 32 rows (0 to 31, 32 to 63, ..., all dimensions but the last counted through in order) at most 3 rows name the same one
Outputs:
- new_left_gram: float32 [4, 96, 512, 512], P('section', 'dp')
- new_right_gram: float32 [4, 96, 512, 512], P('section', 'dp')
- new_left_basis: float32 [4, 96, 512, 512], P('section', 'dp')
- new_right_basis: float32 [4, 96, 512, 512], P('section', 'dp')
- rotated: bfloat16 [4, 96, 512, 512], P('section', 'dp')
The draws below stay inside these ranges and needn't reach their ends.
Inputs may be any that keep to these rules, and one draw needn't show every extreme that they name: `owners`: within one receiving section no device owns more than 3 blocks. `migration`: each row is a permutation of the sections. `left_gram`: each block is symmetric positive definite. `right_gram`: each block is symmetric positive definite.
All inputs are finite; a program needn't handle non-finite values.
Results may differ from the reference program's by a relative error of at most 0.0064.
Values may be sent and summed in bfloat16 or wider, within the bound.
A program may use at most 192 MiB of HBM per device.

```python
import math
import jax
import jax.numpy as jnp
import numpy as np
from jax import lax

BLK = 512
CAP = 3
NB = 32
SLOTS = 96
N_SECTION = 4
N_DP = 32


def spd_blocks(noise, levels):
    sym = (noise + jnp.swapaxes(noise, -1, -2)) * (0.6 / math.sqrt(BLK))
    return sym + levels[..., None] * jnp.eye(BLK, dtype=jnp.float32)


def near_identity(noise):
    return jnp.eye(BLK, dtype=jnp.float32) + noise * (0.35 / math.sqrt(BLK))


def draw_left_gram(key, part):
    key = jax.random.fold_in(key, 11)
    first, second = jax.random.split(key)
    shape = (N_SECTION, NB, BLK, BLK)
    noise = jax.random.truncated_normal(first, -4.0, 4.0, shape, jnp.float32)
    levels = jnp.exp(jax.random.uniform(second, (N_SECTION, NB, BLK), jnp.float32, math.log(2.0), math.log(6.0)))
    return spd_blocks(noise, levels)


def draw_right_gram(key, part):
    key = jax.random.fold_in(key, 12)
    first, second = jax.random.split(key)
    shape = (N_SECTION, NB, BLK, BLK)
    noise = jax.random.truncated_normal(first, -4.0, 4.0, shape, jnp.float32)
    levels = jnp.exp(jax.random.uniform(second, (N_SECTION, NB, BLK), jnp.float32, math.log(2.0), math.log(6.0)))
    return spd_blocks(noise, levels)


def draw_left_basis(key, part):
    key = jax.random.fold_in(key, 13)
    shape = (N_SECTION, NB, BLK, BLK)
    noise = jax.random.truncated_normal(key, -4.0, 4.0, shape, jnp.float32)
    return near_identity(noise)


def draw_right_basis(key, part):
    key = jax.random.fold_in(key, 14)
    shape = (N_SECTION, NB, BLK, BLK)
    noise = jax.random.truncated_normal(key, -4.0, 4.0, shape, jnp.float32)
    return near_identity(noise)


def shard_levels(own_key, dims, shards, smallest, high):
    def one(position, parts):
        heights = jax.random.uniform(jax.random.fold_in(jax.random.fold_in(own_key, 6), position), (parts,), jnp.float32, smallest / len(shards), high / len(shards))
        return jnp.repeat(jnp.exp(heights), dims[position] // parts).reshape((-1,) + (1,) * (len(dims) - position - 1))

    factor_of = one(*shards[0])
    for cut in shards[1:]:
        factor_of = factor_of * one(*cut)
    return factor_of


def shared_out(stream_key, own, number, rows, amount, top, bound, slope):
    ranking = jax.random.permutation(stream_key, amount)
    heavy_load, usual = portions_of(amount, rows * top, bound, slope, True), portions_of(amount, rows * top, bound, slope, False)
    places = jnp.arange(amount)

    def named(tallies, rotation):
        used = int((tallies > 0).sum())
        fixed = max(1, used // 4)
        shifted = fixed + (places - fixed + rotation * (used - fixed)) % max(1, amount - fixed)
        return jnp.zeros((amount,), jnp.int32).at[ranking[jnp.where(places < fixed, places, shifted)]].set(jnp.asarray(tallies, jnp.int32))

    tallies = jnp.where(number % 4 == 0, named(heavy_load, number // 4), named(usual, number - number // 4 - 1))
    mixed = jax.random.permutation(jax.random.fold_in(own, 3), amount)
    source_of, sink = mixed[0:amount // 2 * 2:2], mixed[1:amount // 2 * 2:2]
    slack = jnp.minimum(tallies[source_of] - 1, bound - tallies[sink]) // 2
    slack = jnp.where((source_of == ranking[0]) | (sink == ranking[0]) | (tallies[sink] == 0), 0, jnp.maximum(slack, 0))
    shifted = jax.random.randint(jax.random.fold_in(own, 4), (amount // 2,), 0, 1 << 20) % (slack + 1)
    tallies = tallies.at[source_of].add(-shifted).at[sink].add(shifted)
    labels = jnp.searchsorted(jnp.cumsum(tallies), jnp.arange(rows * top), side="right").astype(jnp.int32)
    grid = labels.reshape(top, rows).T
    grid = grid[jax.random.permutation(jax.random.fold_in(own, 1), rows)]
    rotation = jax.random.randint(jax.random.fold_in(own, 2), (rows, 1), 0, top)
    return jnp.take_along_axis(grid, (jnp.arange(top)[None, :] + rotation) % top, axis=1)


def portions_of(number_of, total, limit, lean, full):
    loads = [(1 << 20) // math.isqrt(rank ** lean) + 1 for rank in range(1, number_of + 1)]
    largest = limit if full else min(limit, max(-(-total // number_of), total * loads[0] // sum(loads)))
    least = 1 if total - largest >= number_of - 1 else 0
    counts, surplus = [largest] + [least] * (number_of - 1), total - largest - least * (number_of - 1)
    while surplus > 0:
        free = [i for i in range(1, number_of) if counts[i] < largest] or [i for i in range(1, number_of) if counts[i] < limit]
        mass, budget = sum([loads[i] for i in free]), surplus
        for i in free:
            extra = min(limit - counts[i], max(1, budget * loads[i] // mass), surplus)
            counts[i] = counts[i] + extra
            surplus = surplus - extra
    return np.array(counts)


def scatter_about(key, shape, width, bound, pieces=(), kind=jnp.bfloat16):
    level = shard_levels(key, shape, pieces, -0.22, 0.18) if pieces else 1.0
    entries = jax.random.normal(key, shape, jnp.float32) * width * level
    return jnp.minimum(jnp.maximum(entries, -bound), bound).astype(kind)


def setup_inputs(seed: int = 0) -> dict:
    key_list = jax.random.split(jax.random.key(seed), 8)
    gradient = scatter_about(key_list[0], (N_SECTION, NB, BLK, BLK), 1.0, 6.0, ((0, 4), (2, 32)))
    left_gram = draw_left_gram(jax.random.fold_in(key_list[7], 71), 0)
    right_gram = draw_right_gram(jax.random.fold_in(key_list[7], 71), 0)
    left_basis = draw_left_basis(jax.random.fold_in(key_list[7], 71), 0)
    right_basis = draw_right_basis(jax.random.fold_in(key_list[7], 71), 0)
    migration = jax.vmap(lambda own: jax.random.permutation(own, N_SECTION))(jax.random.split(key_list[5], N_SECTION)).reshape((N_SECTION, N_SECTION)).astype(jnp.int32)
    owners_keys = jax.random.split(jax.random.fold_in(key_list[6], 1), N_SECTION * NB // NB)
    owners_turns = jax.random.permutation(jax.random.fold_in(key_list[6], 3), N_SECTION * NB // NB)
    owners = jax.vmap(lambda own, number: shared_out(jax.random.fold_in(key_list[6], 2), own, number, NB, N_DP, 1, CAP, 2))(owners_keys, owners_turns).reshape((N_SECTION, NB, 1))
    return dict(gradient=gradient, left_gram=left_gram, right_gram=right_gram, left_basis=left_basis, right_basis=right_basis, migration=migration, owners=owners)


ema_decay = 0.9

def orthonormal(gram, basis):
    highest = lax.Precision.HIGHEST
    power = jnp.dot(gram, basis, precision=highest)
    cross = jnp.dot(power.T, power, precision=highest)
    lower = jnp.linalg.cholesky(cross)
    return jax.scipy.linalg.solve_triangular(lower, power.T, lower=True).T

def refresh(grad, left_old, right_old, lbasis_old, rbasis_old, need_left, need_right):
    scale = (1.0 - ema_decay) / BLK
    left_ema = ema_decay * left_old + scale * jnp.dot(grad.astype(jnp.float32), grad.T.astype(jnp.float32), preferred_element_type=jnp.float32)
    right_ema = ema_decay * right_old + scale * jnp.dot(grad.T.astype(jnp.float32), grad.astype(jnp.float32), preferred_element_type=jnp.float32)
    basis_left = jnp.where(need_left, orthonormal(left_ema, lbasis_old), lbasis_old)
    basis_right = jnp.where(need_right, orthonormal(right_ema, rbasis_old), rbasis_old)
    half = jnp.dot(basis_left.astype(jnp.bfloat16).T.astype(jnp.float32), grad.astype(jnp.float32), preferred_element_type=jnp.float32).astype(jnp.bfloat16)
    turned = jnp.dot(half.astype(jnp.float32), basis_right.astype(jnp.bfloat16).astype(jnp.float32), preferred_element_type=jnp.float32).astype(jnp.bfloat16)
    return (left_ema, right_ema, basis_left, basis_right, turned)

def reference(gradient, left_gram, right_gram, left_basis, right_basis, migration, owners):
    group_size = NB // N_SECTION
    section_ids = jnp.arange(N_SECTION).astype(jnp.int32)
    offsets = jnp.arange(group_size).astype(jnp.int32)
    positions = jnp.arange(NB).astype(jnp.int32)
    need_left = positions % 4 == 0
    need_right = positions % 4 == 2
    collected = [[], [], [], [], []]
    for target in range(N_SECTION):
        source_group = jnp.sum(jnp.where(migration == target, section_ids[None, :], 0), axis=1).astype(jnp.int32)
        source_block = (source_group[:, None] * group_size + offsets[None, :]).reshape(NB).astype(jnp.int32)
        source_section = jnp.repeat(section_ids, group_size).astype(jnp.int32)
        inputs = (gradient[target], left_gram[source_section, source_block], right_gram[source_section, source_block], left_basis[source_section, source_block], right_basis[source_section, source_block], need_left, need_right)
        results = lax.map(lambda items: refresh(*items), inputs)
        listed = owners[target, :, 0].astype(jnp.int32)
        earlier = (listed[None, :] == listed[:, None]) & (positions[None, :] < positions[:, None])
        ranks = jnp.sum(earlier.astype(jnp.int32), axis=1).astype(jnp.int32)
        dest = (listed * CAP + ranks).astype(jnp.int32)
        for index in range(5):
            empty = jnp.zeros((SLOTS, BLK, BLK), results[index].dtype)
            collected[index].append(empty.at[dest].set(results[index]))
    stacked = [jnp.stack(items) for items in collected]
    return (stacked[0], stacked[1], stacked[2], stacked[3], stacked[4])
```

```python
import functools

import jax
import jax.numpy as jnp
from jax import lax
from jax.experimental import pallas as pl
from jax.experimental.pallas import tpu as pltpu
from jax.sharding import PartitionSpec as P

CAP = 3
MESH = pl.DeviceIdType.MESH
bf16, f32 = jnp.bfloat16, jnp.float32
ema_decay = 0.9


def ring_offsets():
    flat = [(0, 0), (0, 1), (1, 0), (0, 3), (3, 0), (1, 1), (3, 3), (1, 3), (3, 1),
            (0, 2), (2, 0), (1, 2), (2, 1), (3, 2), (2, 3), (2, 2)]
    return [(y, z, c) for y, z in flat for c in (0, 1) if (y, z, c) != (0, 0, 0)]


def comm_kernel(group_ref, pick_ref, grad_ref, lg_ref, rg_ref, lb_ref, rb_ref,
                got_g, got_a, got_b,
                xsend, xrecv_a, xrecv_b, send_g, send_a, send_b,
                xs_sem, xr_sem, gs_sem, gr_sem, as_sem, ar_sem, bs_sem, br_sem, own_sem):
    sec = lax.axis_index("section")
    me = lax.axis_index("dp")
    sections, members = 4, 32
    core, z, y = me % 2, (me // 2) % 4, me // 8
    offsets = ring_offsets()

    def partner(off):
        return (((y + off[0]) % 4) * 4 + (z + off[1]) % 4) * 2 + (core + off[2]) % 2

    barrier = pltpu.get_barrier_semaphore()
    for r in range(1, sections):
        pl.semaphore_signal(barrier, inc=1, device_id=((sec + r) % sections, me), device_id_type=MESH)

    def greet(r, _):
        pl.semaphore_signal(barrier, inc=1, device_id=(sec, (me + r) % members), device_id_type=MESH)
        return 0
    lax.fori_loop(1, members, greet, 0)

    def pack(t, to_a, to_b):
        base = group_ref[t] * 8
        for k in range(8):
            first, second = ((lg_ref, lb_ref), (rg_ref, rb_ref))
            if k % 4 >= 2:
                first, second = second, first
            to_a[k, 0] = first[0][base + k].astype(bf16)
            to_a[k, 1] = first[1][base + k].astype(bf16)
            to_b[k, 0] = second[0][base + k].astype(bf16)
            to_b[k, 1] = second[1][base + k].astype(bf16)

    for r in range(1, sections):
        t = (sec + r) % sections
        pack(t, xsend.at[0, r], xsend.at[1, r])
    pack(sec, xrecv_a.at[sec], xrecv_b.at[sec])

    pl.semaphore_wait(barrier, sections - 1 + members - 1)

    xcopies = []
    for half, landing in enumerate((xrecv_a, xrecv_b)):
        for r in (1, 3, 2):
            t = (sec + r) % sections
            xcopies.append(pltpu.make_async_remote_copy(
                src_ref=xsend.at[half, r], dst_ref=landing.at[sec],
                send_sem=xs_sem.at[half, r], recv_sem=xr_sem.at[half, r],
                device_id=(t, me), device_id_type=MESH))
            xcopies[-1].start()

    def slot(o, c):
        j = pick_ref[o * CAP + c]
        return jnp.maximum(j, 0), j >= 0

    def fill_g(o):
        for c in range(CAP):
            j, live = slot(o, c)
            send_g[o, c] = jnp.where(live, grad_ref[j], jnp.zeros((16, 512), bf16))

    def fill_s(ref, held, o):
        for c in range(CAP):
            j, live = slot(o, c)
            for m in range(2):
                ref[o, c, m] = jnp.where(live, held[j // 8, j % 8, m], jnp.zeros((16, 512), bf16))

    def sends(ref, got, s_sem, r_sem, fill):
        copies = []
        for i, off in enumerate(offsets):
            o = partner(off)
            fill(o)
            copies.append(pltpu.make_async_remote_copy(
                src_ref=ref.at[o], dst_ref=got.at[me], send_sem=s_sem.at[i], recv_sem=r_sem.at[i],
                device_id=(sec, o), device_id_type=MESH))
            copies[-1].start()
        fill(me)
        return copies

    copies = sends(send_g, got_g, gs_sem, gr_sem, fill_g)
    for cp in xcopies[:3]:
        cp.wait()
    copies += sends(send_a, got_a, as_sem, ar_sem, lambda o: fill_s(send_a, xrecv_a, o))
    for cp in xcopies[3:]:
        cp.wait()
    copies += sends(send_b, got_b, bs_sem, br_sem, lambda o: fill_s(send_b, xrecv_b, o))
    own = [pltpu.make_async_copy(s.at[me], g.at[me], own_sem.at[i])
           for i, (s, g) in enumerate(((send_g, got_g), (send_a, got_a), (send_b, got_b)))]
    for cp in own:
        cp.start()
    for cp in own:
        cp.wait()
    for cp in copies:
        cp.wait()


def exchange(group, pick, grad, lg, rg, lb, rb):
    members = 32
    vmem = pl.BlockSpec(memory_space=pltpu.VMEM)
    smem = pl.BlockSpec(memory_space=pltpu.SMEM)
    anym = pl.BlockSpec(memory_space=pl.ANY)
    dma = pltpu.SemaphoreType.DMA
    return pl.pallas_call(
        comm_kernel,
        out_shape=[
            jax.ShapeDtypeStruct((members, CAP, 16, 512), bf16),
            jax.ShapeDtypeStruct((members, CAP, 2, 16, 512), bf16),
            jax.ShapeDtypeStruct((members, CAP, 2, 16, 512), bf16),
        ],
        in_specs=[smem, smem] + [vmem] * 5,
        out_specs=[anym] * 3,
        scratch_shapes=[
            pltpu.VMEM((2, 4, 8, 2, 16, 512), bf16),
            pltpu.VMEM((4, 8, 2, 16, 512), bf16),
            pltpu.VMEM((4, 8, 2, 16, 512), bf16),
            pltpu.VMEM((members, CAP, 16, 512), bf16),
            pltpu.VMEM((members, CAP, 2, 16, 512), bf16),
            pltpu.VMEM((members, CAP, 2, 16, 512), bf16),
            dma((2, 4)), dma((2, 4)),
            dma((31,)), dma((31,)), dma((31,)), dma((31,)), dma((31,)), dma((31,)),
            dma((3,)),
        ],
        compiler_params=pltpu.CompilerParams(
            collective_id=0, has_side_effects=True, vmem_limit_bytes=50 << 20),
    )(group, pick, grad, lg, rg, lb, rb)


def dotg(a, b, ca, cb):
    return lax.dot_general(a, b, (((ca,), (cb,)), ((), ())), preferred_element_type=f32)


def split(x):
    high = x.astype(bf16)
    return high, (x - high.astype(f32)).astype(bf16)


def dot3(a, b, ca, cb):
    return dotg(a[0], b[0], ca, cb) + (dotg(a[0], b[1], ca, cb) + dotg(a[1], b[0], ca, cb))


def eliminate(mats, base, m):
    sub = lax.broadcasted_iota(jnp.int32, (8, 128), 0)
    lane = lax.broadcasted_iota(jnp.int32, (8, 128), 1)
    rows_of = [[x[8 * g:8 * g + 8, :] for g in range(8)] for x in mats]
    for k in range(0, 64, m):
        g0, o = k // 8, k % 8
        for a in rows_of:
            b = {g: [jnp.broadcast_to(a[g][:, base + k + i:base + k + i + 1], (8, 128)) for i in range(m)]
                 for g in range(g0, 8)}
            ra = [a[g0][o + i:o + i + 1, :] for i in range(m)]
            c = [[b[g0][i][o + q:o + q + 1, :] for i in range(m)] for q in range(m)]
            inv = []
            for i in range(m):
                inv.append(1.0 / c[i][i])
                for q in range(i + 1, m):
                    l = c[q][i] * inv[i]
                    ra[q] = ra[q] - l * ra[i]
                    for j in range(i + 1, m):
                        c[q][j] = c[q][j] - l * c[i][j]
            for g in range(g0, 8):
                f = []
                for i in range(m):
                    x = b[g][i]
                    for q in range(i):
                        x = x - f[q] * c[q][i]
                    x = x * inv[i]
                    if g == g0:
                        x = jnp.where(sub > o + i, x, 0.0)
                    f.append(x)
                for i in range(m):
                    a[g] = a[g] - f[i] * ra[i]
    keep = (lane < 64) if base == 0 else (lane >= 64)
    out = []
    for a in rows_of:
        rows = []
        for g in range(8):
            d = jnp.sum(jnp.where(lane == sub + (8 * g + base), a[g], 0.0), axis=1, keepdims=True)
            rows.append(jnp.where(keep, pltpu.roll(a[g] * lax.rsqrt(d), 64, 1), 0.0))
        out.append(jnp.concatenate(rows, axis=0))
    return out


def inv_chol(mats, m=4):
    row = lax.broadcasted_iota(jnp.int32, (64, 128), 0)
    lane = lax.broadcasted_iota(jnp.int32, (64, 128), 1)
    low = lane < 64
    m1 = eliminate([jnp.where(low, d[:64], jnp.where(lane == row + 64, 1.0, 0.0)) for d in mats], 0, m)
    m1s = [split(x) for x in m1]
    zero = jnp.zeros((64, 128), f32)
    u, second = [], []
    for s, d in enumerate(mats):
        right = jnp.concatenate([jnp.where(low, 0.0, d[:64]), zero], axis=0)
        u.append(split(dot3(m1s[s], split(right), 1, 0)))
        rest = d[64:] - dot3(u[s], u[s], 0, 0)[64:]
        second.append(jnp.where(low, jnp.where(lane == row, 1.0, 0.0), rest))
    mixed = [split(dot3(u[s], m1s[s], 0, 0)) for s in range(len(mats))]
    m2 = eliminate(second, 64, m)
    return [jnp.concatenate([m1[s], m2[s] - dot3(split(m2[s]), mixed[s], 1, 0)], axis=0)
            for s in range(len(mats))]


def factor(cross, power, fresh):
    for p in range(4):
        lo, hi = 128 * p, 128 * p + 128
        inv = [split(x) for x in inv_chol([cross[s, lo:hi, lo:hi] for s in range(CAP)])]
        if p < 3:
            u = [split(dot3(inv[s], split(cross[s, lo:hi, hi:]), 1, 0)) for s in range(CAP)]
            for s in range(CAP):
                cross[s, hi:, hi:] = cross[s, hi:, hi:] - dot3(u[s], u[s], 0, 0)
        for s in range(CAP):
            q = dot3(split(power[s, :, lo:hi]), inv[s], 1, 1)
            fresh[s, :, lo:hi] = q
            if p < 3:
                power[s, :, hi:] = power[s, :, hi:] - dot3(split(q), u[s], 1, 0)


def refresh_kernel(left_ref, need_ref, got_g, got_a, got_b,
                   out_lg, out_rg, out_lb, out_rb, out_rot,
                   g_in, a_in, b_in, ema, basis, turned, cross, power, in_sem, out_sem):
    loads = []
    for c in range(CAP):
        todo = [(got_g.at[:, c], g_in.at[c])]
        todo += [(got_a.at[:, c, m], a_in.at[c, m]) for m in range(2)]
        todo += [(got_b.at[:, c, m], b_in.at[c, m]) for m in range(2)]
        loads.append([pltpu.make_async_copy(src, dst, in_sem.at[c, i]) for i, (src, dst) in enumerate(todo)])
    for i in range(5):
        for c in range(CAP):
            loads[c][i].start()

    scale = (1.0 - ema_decay) / 512.0
    size = (512, 512)

    def put(c, kind, src, mine, other, flag):
        @pl.when(flag)
        def _():
            pltpu.make_async_copy(src, mine.at[c], out_sem.at[c, kind]).start()

        @pl.when(jnp.logical_not(flag))
        def _():
            pltpu.make_async_copy(src, other.at[c], out_sem.at[c, kind]).start()

    for c in range(CAP):
        is_left = left_ref[c] > 0
        need = need_ref[c] > 0
        loads[c][0].wait()
        g = g_in[c].reshape(size)
        outer = dotg(g, g, 1, 1)
        inner = dotg(g, g, 0, 0)
        loads[c][1].wait()
        here = ema_decay * a_in[c, 0].reshape(size).astype(f32) + scale * jnp.where(is_left, outer, inner)
        ema[c, 0] = here
        put(c, 0, ema.at[c, 0], out_lg, out_rg, is_left)
        loads[c][3].wait()
        ema[c, 1] = ema_decay * b_in[c, 0].reshape(size).astype(f32) + scale * jnp.where(is_left, inner, outer)
        put(c, 1, ema.at[c, 1], out_rg, out_lg, is_left)
        loads[c][2].wait()
        held = split(ema[c, 0])
        old = a_in[c, 1].reshape(size)
        grown = dotg(held[0], old, 1, 0) + dotg(held[1], old, 1, 0)
        power[c] = grown
        ps = split(grown)
        eye = (lax.broadcasted_iota(jnp.int32, size, 0) == lax.broadcasted_iota(jnp.int32, size, 1)).astype(f32)
        cross[c] = jnp.where(need, dot3(ps, ps, 0, 0), eye)
        loads[c][4].wait()
        basis[c, 1] = b_in[c, 1].reshape(size).astype(f32)
        put(c, 3, basis.at[c, 1], out_rb, out_lb, is_left)

    factor(cross, power, basis.at[:, 0])

    for c in range(CAP):
        is_left = left_ref[c] > 0
        need = need_ref[c] > 0
        first = jnp.where(need, basis[c, 0], a_in[c, 1].reshape(size).astype(f32))
        basis[c, 0] = first
        put(c, 2, basis.at[c, 0], out_lb, out_rb, is_left)
        first = first.astype(bf16)
        second = b_in[c, 1].reshape(size)
        low_left = jnp.where(is_left, first, second)
        low_right = jnp.where(is_left, second, first)
        half = dotg(low_left, g_in[c].reshape(size), 0, 0).astype(bf16)
        turned[c] = dotg(half, low_right, 1, 0).astype(bf16)
        pltpu.make_async_copy(turned.at[c], out_rot.at[c], out_sem.at[c, 4]).start()
    for c in range(CAP):
        pltpu.make_async_copy(ema.at[c, 0], out_lg.at[c], out_sem.at[c, 0]).wait()
        pltpu.make_async_copy(ema.at[c, 1], out_rg.at[c], out_sem.at[c, 1]).wait()
        pltpu.make_async_copy(basis.at[c, 0], out_lb.at[c], out_sem.at[c, 2]).wait()
        pltpu.make_async_copy(basis.at[c, 1], out_rb.at[c], out_sem.at[c, 3]).wait()
        pltpu.make_async_copy(turned.at[c], out_rot.at[c], out_sem.at[c, 4]).wait()


def refresh(is_left, need, got_g, got_a, got_b):
    smem = pl.BlockSpec(memory_space=pltpu.SMEM)
    anym = pl.BlockSpec(memory_space=pl.ANY)
    full = jax.ShapeDtypeStruct((CAP, 512, 512), f32)
    return pl.pallas_call(
        refresh_kernel,
        out_shape=[full] * 4 + [jax.ShapeDtypeStruct((CAP, 512, 512), bf16)],
        in_specs=[smem, smem] + [anym] * 3,
        out_specs=[anym] * 5,
        scratch_shapes=[
            pltpu.VMEM((CAP, 32, 16, 512), bf16),
            pltpu.VMEM((CAP, 2, 32, 16, 512), bf16),
            pltpu.VMEM((CAP, 2, 32, 16, 512), bf16),
            pltpu.VMEM((CAP, 2, 512, 512), f32),
            pltpu.VMEM((CAP, 2, 512, 512), f32),
            pltpu.VMEM((CAP, 512, 512), bf16),
            pltpu.VMEM((CAP, 512, 512), f32),
            pltpu.VMEM((CAP, 512, 512), f32),
            pltpu.SemaphoreType.DMA((CAP, 5)),
            pltpu.SemaphoreType.DMA((CAP, 5)),
        ],
        compiler_params=pltpu.CompilerParams(vmem_limit_bytes=56 << 20),
    )(is_left, need, got_g, got_a, got_b)


def shards(gradient, left_gram, right_gram, left_basis, right_basis, migration, owners):
    sections = lax.axis_size("section")
    members = lax.axis_size("dp")
    blocks = gradient.shape[1]
    here_section = lax.axis_index("section")
    here_member = lax.axis_index("dp")
    own_row = lax.dynamic_index_in_dim(migration, here_section, 0, keepdims=False)
    targets = jnp.arange(sections, dtype=jnp.int32)
    send_group = jnp.sum(jnp.where(own_row[None, :] == targets[:, None], targets[None, :], 0), axis=1)
    listed = lax.dynamic_index_in_dim(owners, here_section, 0, keepdims=False)[:, 0]
    positions = jnp.arange(blocks, dtype=jnp.int32)
    earlier = (listed[None, :] == listed[:, None]) & (positions[None, :] < positions[:, None])
    ranks = jnp.sum(earlier.astype(jnp.int32), axis=1)
    places = listed * CAP + ranks
    slots = jnp.arange(members * CAP, dtype=jnp.int32)
    pick = jnp.sum(jnp.where(places[None, :] == slots[:, None], positions[None, :] + 1, 0), axis=1) - 1
    mine = lax.dynamic_slice_in_dim(pick, here_member * CAP, CAP)
    is_left = ((mine >= 0) & (mine % 4 < 2)).astype(jnp.int32)
    need = ((mine >= 0) & (mine % 2 == 0)).astype(jnp.int32)
    got = exchange(send_group, pick, gradient[0], left_gram[0], right_gram[0], left_basis[0], right_basis[0])
    outs = refresh(is_left, need, *got)
    return tuple(o[None] for o in outs)


def solution(mesh):
    in_specs = (P("section", None, "dp", None),) * 5 + (P(), P())
    out_specs = (P("section", "dp", None, None),) * 5
    return jax.shard_map(shards, mesh=mesh, in_specs=in_specs, out_specs=out_specs, check_vma=False)
```

```python
import functools

import jax
import jax.numpy as jnp
from jax import lax
from jax.experimental import pallas as pl
from jax.experimental.pallas import tpu as pltpu
from jax.sharding import PartitionSpec as P

CAP = 3
MESH = pl.DeviceIdType.MESH
bf16, f32 = jnp.bfloat16, jnp.float32
ema_decay = 0.9


def dotg(a, b, ca, cb):
    return lax.dot_general(a, b, (((ca,), (cb,)), ((), ())), preferred_element_type=f32)


def split(x):
    high = x.astype(bf16)
    return high, (x - high.astype(f32)).astype(bf16)


def dot3(a, b, ca, cb):
    return dotg(a[0], b[0], ca, cb) + (dotg(a[0], b[1], ca, cb) + dotg(a[1], b[0], ca, cb))


def eliminate(mats, base, m):
    sub = lax.broadcasted_iota(jnp.int32, (8, 128), 0)
    row = lax.broadcasted_iota(jnp.int32, (64, 128), 0)
    lane = lax.broadcasted_iota(jnp.int32, (64, 128), 1)
    left = list(mats)
    done = [[] for _ in mats]
    for k in range(0, 64, m):
        o = k % 8
        for s in range(len(mats)):
            a = left[s]
            n = a.shape[0]
            at = base + k
            b = [jnp.broadcast_to(a[:, at + i:at + i + 1], (n, 128)) for i in range(m)]
            ra = [a[o + i:o + i + 1, :] for i in range(m)]
            c = [[b[i][o + q:o + q + 1, :] for i in range(m)] for q in range(m)]
            inv = []
            for i in range(m):
                inv.append(1.0 / c[i][i])
                for q in range(i + 1, m):
                    l = c[q][i] * inv[i]
                    ra[q] = ra[q] - l * ra[i]
                    for j in range(i + 1, m):
                        c[q][j] = c[q][j] - l * c[i][j]
            f = []
            for i in range(m):
                x = b[i]
                for q in range(i):
                    x = x - f[q] * c[q][i]
                x = x * inv[i]
                top = jnp.where(sub > o + i, x[:8], 0.0)
                f.append(top if n == 8 else jnp.concatenate([top, x[8:]], axis=0))
            for i in range(m):
                a = a - f[i] * ra[i]
            if o + m == 8:
                done[s].append(a[:8])
                a = a[8:]
            left[s] = a
    keep = (lane < 64) if base == 0 else (lane >= 64)
    out = []
    for s in range(len(mats)):
        a = jnp.concatenate(done[s], axis=0)
        d = jnp.sum(jnp.where(lane == row + base, a, 0.0), axis=1, keepdims=True)
        out.append(jnp.where(keep, pltpu.roll(a * lax.rsqrt(d), 64, 1), 0.0))
    return out


def inv_chol(mats, m=4):
    row = lax.broadcasted_iota(jnp.int32, (64, 128), 0)
    lane = lax.broadcasted_iota(jnp.int32, (64, 128), 1)
    low = lane < 64
    m1 = eliminate([jnp.where(low, d[:64], jnp.where(lane == row + 64, 1.0, 0.0)) for d in mats], 0, m)
    m1s = [split(x) for x in m1]
    zero = jnp.zeros((64, 128), f32)
    u, second = [], []
    for s, d in enumerate(mats):
        right = jnp.concatenate([jnp.where(low, 0.0, d[:64]), zero], axis=0)
        u.append(split(dot3(m1s[s], split(right), 1, 0)))
        rest = d[64:] - dot3(u[s], u[s], 0, 0)[64:]
        second.append(jnp.where(low, jnp.where(lane == row, 1.0, 0.0), rest))
    mixed = [split(dot3(u[s], m1s[s], 0, 0)) for s in range(len(mats))]
    m2 = eliminate(second, 64, m)
    return [jnp.concatenate([m1[s], m2[s] - dot3(split(m2[s]), mixed[s], 1, 0)], axis=0)
            for s in range(len(mats))]


def factor(cross, power, fresh):
    for p in range(4):
        lo, hi = 128 * p, 128 * p + 128
        inv = [split(x) for x in inv_chol([cross[s, lo:hi, lo:hi] for s in range(CAP)])]
        if p < 3:
            u = [split(dot3(inv[s], split(cross[s, lo:hi, hi:]), 1, 0)) for s in range(CAP)]
            for s in range(CAP):
                cross[s, hi:, hi:] = cross[s, hi:, hi:] - dot3(u[s], u[s], 0, 0)
        for s in range(CAP):
            q = dot3(split(power[s, :, lo:hi]), inv[s], 1, 1)
            fresh[s, :, lo:hi] = q
            if p < 3:
                power[s, :, hi:] = power[s, :, hi:] - dot3(split(q), u[s], 1, 0)


def partner_offsets():
    chips = [(2, 2), (1, 2), (3, 2), (2, 1), (2, 3), (1, 1), (3, 3), (1, 3), (3, 1), (0, 2), (2, 0),
             (0, 1), (1, 0), (0, 3), (3, 0)]
    return [chip + (c,) for chip in chips for c in (0, 1)] + [(0, 0, 1)]


def exchange_kernel(group_ref, pick_ref, left_ref, need_ref, grad_hbm, lg_hbm, rg_hbm, lb_hbm, rb_hbm,
                    got_g, got_a, got_b, fresh_hbm,
                    grad_ref, state, xsend, xrecv_a, xrecv_b, send_g, send_a, send_b,
                    land_g, land_a, cross, power, fresh,
                    in_sem, xs_sem, xr_sem, gs_sem, gr_sem, as_sem, ar_sem, bs_sem, br_sem, out_sem):
    sec = lax.axis_index("section")
    me = lax.axis_index("dp")
    sections, members = 4, 32
    core, z, y = me % 2, (me // 2) % 4, me // 8
    partners = [(((y + off[0]) % 4) * 4 + (z + off[1]) % 4) * 2 + (core + off[2]) % 2
                for off in partner_offsets()]
    size = (512, 512)
    blank = jnp.zeros((16, 512), bf16)

    fetches = [pltpu.make_async_copy(src, state.at[i], in_sem.at[i])
               for i, src in enumerate((lg_hbm, lb_hbm, rg_hbm, rb_hbm))]
    fetches.append(pltpu.make_async_copy(grad_hbm, grad_ref, in_sem.at[4]))
    for cp in fetches:
        cp.start()

    barrier = pltpu.get_barrier_semaphore()
    for r in range(1, sections):
        pl.semaphore_signal(barrier, inc=1, device_id=((sec + r) % sections, me), device_id_type=MESH)

    def greet(r, _):
        pl.semaphore_signal(barrier, inc=1, device_id=(sec, (me + r) % members), device_id_type=MESH)
        return 0
    lax.fori_loop(1, members, greet, 0)

    def pack(t, half, to_ref):
        base = group_ref[t] * 8
        for k in range(8):
            side = (k % 4 >= 2) != (half == 1)
            for m in range(2):
                to_ref[k, m] = state[2 * side + m, base + k].astype(bf16)

    def xsends(half, landing):
        copies = []
        for r in (2, 1, 3):
            t = (sec + r) % sections
            copies.append(pltpu.make_async_remote_copy(
                src_ref=xsend.at[half, r], dst_ref=landing.at[sec],
                send_sem=xs_sem.at[half, r], recv_sem=xr_sem.at[half, r],
                device_id=(t, me), device_id_type=MESH))
            copies[-1].start()
        return copies

    for cp in fetches[:4]:
        cp.wait()
    for r in range(1, sections):
        pack((sec + r) % sections, 0, xsend.at[0, r])
    pl.semaphore_wait(barrier, sections - 1 + members - 1)
    xcopies_a = xsends(0, xrecv_a)
    fetches[4].wait()

    def slot(o, c):
        j = pick_ref[o * CAP + c]
        return jnp.maximum(j, 0), j >= 0

    def sends(ref_of, got, s_sem, r_sem):
        copies = []
        for i, o in enumerate(partners):
            copies.append(pltpu.make_async_remote_copy(
                src_ref=ref_of(o), dst_ref=got, send_sem=s_sem.at[i], recv_sem=r_sem.at[i],
                device_id=(sec, o), device_id_type=MESH))
        return copies

    def fill_g(o, to_ref):
        for c in range(CAP):
            j, live = slot(o, c)
            to_ref[c] = jnp.where(live, grad_ref[j], blank)

    copies_g = sends(lambda o: send_g.at[o], land_g.at[me], gs_sem, gr_sem)
    for o, cp in zip(partners, copies_g):
        fill_g(o, send_g.at[o])
        cp.start()
    fill_g(me, land_g.at[me])

    for r in range(1, sections):
        pack((sec + r) % sections, 1, xsend.at[1, r])
    xcopies_b = xsends(1, xrecv_b)
    pack(sec, 0, xrecv_a.at[sec])
    pack(sec, 1, xrecv_b.at[sec])

    def fill_s(held, o, c, to_ref):
        j, live = slot(o, c)
        for m in range(2):
            to_ref[m] = jnp.where(live, held[j // 8, j % 8, m], blank)

    for cp in xcopies_a:
        cp.wait()
    copies_a = []
    for c in range(CAP):
        copies_a.append(sends(lambda o: send_a.at[c, o], land_a.at[c, me], as_sem.at[c], ar_sem.at[c]))
        for o, cp in zip(partners, copies_a[c]):
            fill_s(xrecv_a, o, c, send_a.at[c, o])
            cp.start()
        fill_s(xrecv_a, me, c, land_a.at[c, me])

    for cp in xcopies_b:
        cp.wait()
    for i, o in enumerate(partners + [me]):
        for c in range(CAP):
            fill_s(xrecv_b, o, c, send_b.at[o, c])
    copies_b = sends(lambda o: send_b.at[o], got_b.at[me], bs_sem, br_sem)
    own_b = pltpu.make_async_copy(send_b.at[me], got_b.at[me], out_sem.at[0])
    own_b.start()

    scale = (1.0 - ema_decay) / 512.0

    def prepare(c):
        g = land_g[:, c].reshape(size)
        outer = dotg(g, g, 1, 1)
        inner = dotg(g, g, 0, 0)
        gram = land_a[c, :, 0].reshape(size).astype(f32)
        ema = split(ema_decay * gram + scale * jnp.where(left_ref[c] > 0, outer, inner))
        old = land_a[c, :, 1].reshape(size)
        grown = dotg(ema[0], old, 1, 0) + dotg(ema[1], old, 1, 0)
        power[c] = grown
        ps = split(grown)
        eye = (lax.broadcasted_iota(jnp.int32, size, 0) == lax.broadcasted_iota(jnp.int32, size, 1)).astype(f32)
        cross[c] = jnp.where(need_ref[c] > 0, dot3(ps, ps, 0, 0), eye)

    for cp in copies_g:
        cp.wait()
    for c in range(CAP):
        if c == CAP - 1:
            for copies in copies_a:
                for cp in copies:
                    cp.wait_send()
            for cp in copies_b:
                cp.start()
        for cp in copies_a[c]:
            cp.wait_recv()
        prepare(c)
    outs = [pltpu.make_async_copy(land_g, got_g, out_sem.at[1]), pltpu.make_async_copy(land_a, got_a, out_sem.at[2])]
    for cp in outs:
        cp.start()
    factor(cross, power, fresh)
    outs.append(pltpu.make_async_copy(fresh, fresh_hbm, out_sem.at[3]))
    outs[-1].start()
    own_b.wait()
    for cp in outs:
        cp.wait()
    for cp in copies_b:
        cp.wait()


def exchange(group, pick, is_left, need, grad, lg, rg, lb, rb):
    members = 32
    smem = pl.BlockSpec(memory_space=pltpu.SMEM)
    anym = pl.BlockSpec(memory_space=pl.ANY)
    dma = pltpu.SemaphoreType.DMA
    return pl.pallas_call(
        exchange_kernel,
        out_shape=[
            jax.ShapeDtypeStruct((members, CAP, 16, 512), bf16),
            jax.ShapeDtypeStruct((CAP, members, 2, 16, 512), bf16),
            jax.ShapeDtypeStruct((members, CAP, 2, 16, 512), bf16),
            jax.ShapeDtypeStruct((CAP, 512, 512), f32),
        ],
        in_specs=[smem] * 4 + [anym] * 5,
        out_specs=[anym] * 4,
        scratch_shapes=[
            pltpu.VMEM((32, 16, 512), bf16),
            pltpu.VMEM((4, 32, 16, 512), f32),
            pltpu.VMEM((2, 4, 8, 2, 16, 512), bf16),
            pltpu.VMEM((4, 8, 2, 16, 512), bf16),
            pltpu.VMEM((4, 8, 2, 16, 512), bf16),
            pltpu.VMEM((members, CAP, 16, 512), bf16),
            pltpu.VMEM((CAP, members, 2, 16, 512), bf16),
            pltpu.VMEM((members, CAP, 2, 16, 512), bf16),
            pltpu.VMEM((members, CAP, 16, 512), bf16),
            pltpu.VMEM((CAP, members, 2, 16, 512), bf16),
            pltpu.VMEM((CAP, 512, 512), f32),
            pltpu.VMEM((CAP, 512, 512), f32),
            pltpu.VMEM((CAP, 512, 512), f32),
            dma((5,)), dma((2, 4)), dma((2, 4)),
            dma((31,)), dma((31,)), dma((CAP, 31)), dma((CAP, 31)), dma((31,)), dma((31,)),
            dma((4,)),
        ],
        compiler_params=pltpu.CompilerParams(
            collective_id=0, has_side_effects=True, vmem_limit_bytes=56 << 20),
    )(group, pick, is_left, need, grad, lg, rg, lb, rb)


def finish_kernel(left_ref, need_ref, got_g, got_a, got_b, fresh_hbm,
                  out_lg, out_rg, out_lb, out_rb, out_rot,
                  g_in, a_in, b_in, fresh, ema, basis, turned, in_sem, out_sem):
    loads = []
    for c in range(CAP):
        todo = [(got_g.at[:, c], g_in.at[c]), (got_a.at[c], a_in.at[c]), (got_b.at[:, c], b_in.at[c]),
                (fresh_hbm.at[c], fresh.at[c])]
        loads.append([pltpu.make_async_copy(src, dst, in_sem.at[c, i]) for i, (src, dst) in enumerate(todo)])
        for cp in loads[c]:
            cp.start()

    scale = (1.0 - ema_decay) / 512.0
    size = (512, 512)

    def put(c, kind, src, mine, other, flag):
        @pl.when(flag)
        def _():
            pltpu.make_async_copy(src, mine.at[c], out_sem.at[c, kind]).start()

        @pl.when(jnp.logical_not(flag))
        def _():
            pltpu.make_async_copy(src, other.at[c], out_sem.at[c, kind]).start()

    for c in range(CAP):
        is_left = left_ref[c] > 0
        need = need_ref[c] > 0
        for cp in loads[c]:
            cp.wait()
        basis[c, 1] = b_in[c, :, 1].reshape(size).astype(f32)
        put(c, 3, basis.at[c, 1], out_rb, out_lb, is_left)
        first = jnp.where(need, fresh[c], a_in[c, :, 1].reshape(size).astype(f32))
        basis[c, 0] = first
        put(c, 2, basis.at[c, 0], out_lb, out_rb, is_left)
        g = g_in[c].reshape(size)
        outer = dotg(g, g, 1, 1)
        inner = dotg(g, g, 0, 0)
        ema[c, 0] = (ema_decay * a_in[c, :, 0].reshape(size).astype(f32)
                     + scale * jnp.where(is_left, outer, inner))
        put(c, 0, ema.at[c, 0], out_lg, out_rg, is_left)
        ema[c, 1] = (ema_decay * b_in[c, :, 0].reshape(size).astype(f32)
                     + scale * jnp.where(is_left, inner, outer))
        put(c, 1, ema.at[c, 1], out_rg, out_lg, is_left)
        first = first.astype(bf16)
        second = b_in[c, :, 1].reshape(size)
        low_left = jnp.where(is_left, first, second)
        low_right = jnp.where(is_left, second, first)
        half = dotg(low_left, g, 0, 0).astype(bf16)
        turned[c] = dotg(half, low_right, 1, 0).astype(bf16)
        pltpu.make_async_copy(turned.at[c], out_rot.at[c], out_sem.at[c, 4]).start()
    for c in range(CAP):
        pltpu.make_async_copy(ema.at[c, 0], out_lg.at[c], out_sem.at[c, 0]).wait()
        pltpu.make_async_copy(ema.at[c, 1], out_rg.at[c], out_sem.at[c, 1]).wait()
        pltpu.make_async_copy(basis.at[c, 0], out_lb.at[c], out_sem.at[c, 2]).wait()
        pltpu.make_async_copy(basis.at[c, 1], out_rb.at[c], out_sem.at[c, 3]).wait()
        pltpu.make_async_copy(turned.at[c], out_rot.at[c], out_sem.at[c, 4]).wait()


def finish(is_left, need, got_g, got_a, got_b, fresh):
    smem = pl.BlockSpec(memory_space=pltpu.SMEM)
    anym = pl.BlockSpec(memory_space=pl.ANY)
    full = jax.ShapeDtypeStruct((CAP, 512, 512), f32)
    return pl.pallas_call(
        finish_kernel,
        out_shape=[full] * 4 + [jax.ShapeDtypeStruct((CAP, 512, 512), bf16)],
        in_specs=[smem, smem] + [anym] * 4,
        out_specs=[anym] * 5,
        scratch_shapes=[
            pltpu.VMEM((CAP, 32, 16, 512), bf16),
            pltpu.VMEM((CAP, 32, 2, 16, 512), bf16),
            pltpu.VMEM((CAP, 32, 2, 16, 512), bf16),
            pltpu.VMEM((CAP, 512, 512), f32),
            pltpu.VMEM((CAP, 2, 512, 512), f32),
            pltpu.VMEM((CAP, 2, 512, 512), f32),
            pltpu.VMEM((CAP, 512, 512), bf16),
            pltpu.SemaphoreType.DMA((CAP, 4)),
            pltpu.SemaphoreType.DMA((CAP, 5)),
        ],
        compiler_params=pltpu.CompilerParams(vmem_limit_bytes=56 << 20),
    )(is_left, need, got_g, got_a, got_b, fresh)


def shards(gradient, left_gram, right_gram, left_basis, right_basis, migration, owners):
    sections = lax.axis_size("section")
    members = lax.axis_size("dp")
    blocks = gradient.shape[1]
    here_section = lax.axis_index("section")
    here_member = lax.axis_index("dp")
    own_row = lax.dynamic_index_in_dim(migration, here_section, 0, keepdims=False)
    targets = jnp.arange(sections, dtype=jnp.int32)
    send_group = jnp.sum(jnp.where(own_row[None, :] == targets[:, None], targets[None, :], 0), axis=1)
    listed = lax.dynamic_index_in_dim(owners, here_section, 0, keepdims=False)[:, 0]
    positions = jnp.arange(blocks, dtype=jnp.int32)
    earlier = (listed[None, :] == listed[:, None]) & (positions[None, :] < positions[:, None])
    ranks = jnp.sum(earlier.astype(jnp.int32), axis=1)
    places = listed * CAP + ranks
    slots = jnp.arange(members * CAP, dtype=jnp.int32)
    pick = jnp.sum(jnp.where(places[None, :] == slots[:, None], positions[None, :] + 1, 0), axis=1) - 1
    mine = lax.dynamic_slice_in_dim(pick, here_member * CAP, CAP)
    is_left = ((mine >= 0) & (mine % 4 < 2)).astype(jnp.int32)
    need = ((mine >= 0) & (mine % 2 == 0)).astype(jnp.int32)
    got = exchange(send_group, pick, is_left, need,
                   gradient[0], left_gram[0], right_gram[0], left_basis[0], right_basis[0])
    outs = finish(is_left, need, *got)
    return tuple(o[None] for o in outs)


def solution(mesh):
    in_specs = (P("section", None, "dp", None),) * 5 + (P(), P())
    out_specs = (P("section", "dp", None, None),) * 5
    return jax.shard_map(shards, mesh=mesh, in_specs=in_specs, out_specs=out_specs, check_vma=False)
```

```python
import functools

import jax
import jax.numpy as jnp
from jax import lax
from jax.experimental import pallas as pl
from jax.experimental.pallas import tpu as pltpu
from jax.sharding import PartitionSpec as P

CAP = 3
MESH = pl.DeviceIdType.MESH
bf16, f32 = jnp.bfloat16, jnp.float32
ema_decay = 0.9


def dotg(a, b, ca, cb):
    return lax.dot_general(a, b, (((ca,), (cb,)), ((), ())), preferred_element_type=f32)


def split(x):
    high = x.astype(bf16)
    return high, (x - high.astype(f32)).astype(bf16)


def dot3(a, b, ca, cb):
    return dotg(jnp.concatenate([a[0], a[0], a[1]], axis=ca), jnp.concatenate([b[0], b[1], b[0]], axis=cb), ca, cb)


def eliminate(mats, base, m):
    sub = lax.broadcasted_iota(jnp.int32, (8, 128), 0)
    row = lax.broadcasted_iota(jnp.int32, (64, 128), 0)
    lane = lax.broadcasted_iota(jnp.int32, (64, 128), 1)
    left = list(mats)
    done = [[] for _ in mats]
    for k in range(0, 64, m):
        o = k % 8
        for s in range(len(mats)):
            a = left[s]
            n = a.shape[0]
            at = base + k
            b = [jnp.broadcast_to(a[:, at + i:at + i + 1], (n, 128)) for i in range(m)]
            ra = [a[o + i:o + i + 1, :] for i in range(m)]
            c = [[b[i][o + q:o + q + 1, :] for i in range(m)] for q in range(m)]
            inv = []
            for i in range(m):
                inv.append(1.0 / c[i][i])
                for q in range(i + 1, m):
                    l = c[q][i] * inv[i]
                    ra[q] = ra[q] - l * ra[i]
                    for j in range(i + 1, m):
                        c[q][j] = c[q][j] - l * c[i][j]
            f = []
            for i in range(m):
                x = b[i]
                for q in range(i):
                    x = x - f[q] * c[q][i]
                x = x * inv[i]
                top = jnp.where(sub > o + i, x[:8], 0.0)
                f.append(top if n == 8 else jnp.concatenate([top, x[8:]], axis=0))
            for i in range(m):
                a = a - f[i] * ra[i]
            if o + m == 8:
                done[s].append(a[:8])
                a = a[8:]
            left[s] = a
    keep = (lane < 64) if base == 0 else (lane >= 64)
    out = []
    for s in range(len(mats)):
        a = jnp.concatenate(done[s], axis=0)
        d = jnp.sum(jnp.where(lane == row + base, a, 0.0), axis=1, keepdims=True)
        out.append(jnp.where(keep, pltpu.roll(a * lax.rsqrt(d), 64, 1), 0.0))
    return out


def inv_chol(mats, m=4):
    row = lax.broadcasted_iota(jnp.int32, (64, 128), 0)
    lane = lax.broadcasted_iota(jnp.int32, (64, 128), 1)
    low = lane < 64
    m1 = eliminate([jnp.where(low, d[:64], jnp.where(lane == row + 64, 1.0, 0.0)) for d in mats], 0, m)
    m1s = [split(x) for x in m1]
    zero = jnp.zeros((64, 128), f32)
    u, second = [], []
    for s, d in enumerate(mats):
        right = jnp.concatenate([jnp.where(low, 0.0, d[:64]), zero], axis=0)
        u.append(split(dot3(m1s[s], split(right), 1, 0)))
        rest = d[64:] - dot3(u[s], u[s], 0, 0)[64:]
        second.append(jnp.where(low, jnp.where(lane == row, 1.0, 0.0), rest))
    mixed = [split(dot3(u[s], m1s[s], 0, 0)) for s in range(len(mats))]
    m2 = eliminate(second, 64, m)
    return [jnp.concatenate([m1[s], m2[s] - dot3(split(m2[s]), mixed[s], 1, 0)], axis=0)
            for s in range(len(mats))]


def factor_panel(p, cross, power, fresh, count):
    at = pl.ds(pl.multiple_of(p * 128, 128), 128)
    inv = [split(x) for x in inv_chol([cross[s, at, at] for s in range(count)])]
    new = [dot3(split(power[s, :, at]), inv[s], 1, 1) for s in range(count)]
    for s in range(count):
        fresh[p, s] = new[s].astype(bf16)

    def rest(lo, hi):
        u = [split(dot3(inv[s], split(cross[s, lo:hi, hi:]), 1, 0)) for s in range(count)]
        for s in range(count):
            cross[s, hi:, hi:] = cross[s, hi:, hi:] - dot3(u[s], u[s], 0, 0)
            power[s, :, hi:] = power[s, :, hi:] - dot3(split(new[s]), u[s], 1, 0)

    for k in range(3):
        pl.when(p == k)(functools.partial(rest, 128 * k, 128 * k + 128))


CHIP = 6
CHIPS = 16
FAR_FIRST = [(2, 2), (1, 2), (3, 2), (2, 1), (2, 3), (1, 1), (3, 3), (1, 3), (3, 1), (0, 2), (2, 0),
             (0, 1), (1, 0), (0, 3), (3, 0)]


def exchange_kernel(slots, group_ref, table_ref, grad_hbm, lg_hbm, rg_hbm, lb_hbm, rb_hbm,
                    got_g, got_a, got_b, got_f,
                    grad_ref, state, xsend, xrecv_a, xrecv_b, send_g, send_a, send_b,
                    land_g, land_a, sums, cross, power, fresh,
                    in_sem, xs_sem, xr_sem, gs_sem, gr_sem, as_sem, ar_sem, bs_sem, br_sem,
                    gfs_sem, gfr_sem, afs_sem, afr_sem, bfs_sem, bfr_sem, ffs_sem, ffr_sem, out_sem):
    sec = lax.axis_index("section")
    me = lax.axis_index("dp")
    sections = 4
    count = slots // 2
    core, z, y = me % 2, (me // 2) % 4, me // 8
    chip = me // 2
    sibling = chip * 2 + 1 - core
    chips = [((y + off[0]) % 4) * 4 + (z + off[1]) % 4 for off in FAR_FIRST]
    back = [((y + 4 - off[0]) % 4) * 4 + (z + 4 - off[1]) % 4 for off in FAR_FIRST]
    size = (512, 512)
    blank = jnp.zeros((16, 512), bf16)
    every = pl.ds(0, slots)

    fetches = [pltpu.make_async_copy(src, state.at[i], in_sem.at[i])
               for i, src in enumerate((lg_hbm, lb_hbm, rg_hbm, rb_hbm))]
    fetches.append(pltpu.make_async_copy(grad_hbm, grad_ref, in_sem.at[4]))
    for cp in fetches:
        cp.start()

    barrier = pltpu.get_barrier_semaphore()
    for r in range(1, sections):
        pl.semaphore_signal(barrier, inc=1, device_id=((sec + r) % sections, me), device_id_type=MESH)
    pl.semaphore_signal(barrier, inc=1, device_id=(sec, sibling), device_id_type=MESH)
    for o in chips:
        pl.semaphore_signal(barrier, inc=1, device_id=(sec, o * 2 + core), device_id_type=MESH)

    def pack(t, half, to_ref):
        base = group_ref[t] * 8
        for k in range(8):
            side = (k % 4 >= 2) != (half == 1)
            for m in range(2):
                to_ref[k, m] = state[2 * side + m, base + k].astype(bf16)

    def xsends(half, landing):
        copies = []
        for r in (2, 1, 3):
            t = (sec + r) % sections
            copies.append(pltpu.make_async_remote_copy(
                src_ref=xsend.at[half, r], dst_ref=landing.at[sec],
                send_sem=xs_sem.at[half, r], recv_sem=xr_sem.at[half, r],
                device_id=(t, me), device_id_type=MESH))
            copies[-1].start()
        return copies

    for cp in fetches[:4]:
        cp.wait()
    for r in range(1, sections):
        pack((sec + r) % sections, 0, xsend.at[0, r])
    pl.semaphore_wait(barrier, sections - 1 + 1 + len(chips))
    xcopies_a = xsends(0, xrecv_a)
    fetches[4].wait()

    def block(o, q):
        j = table_ref[o * CHIP + q] % 64 - 1
        return jnp.maximum(j, 0), j >= 0

    def sends(ref, got, s_sem, r_sem):
        copies = []
        for i, (o, c) in enumerate([(o, core) for o in chips] + [(chip, 1 - core)]):
            copies.append(pltpu.make_async_remote_copy(
                src_ref=ref.at[o], dst_ref=got, send_sem=s_sem.at[i], recv_sem=r_sem.at[i],
                device_id=(sec, o * 2 + c), device_id_type=MESH))
        return copies

    def forwards(got, s_sem, r_sem):
        copies = []
        for i, o in enumerate(back):
            copies.append(pltpu.make_async_remote_copy(
                src_ref=got(o * 2 + core), dst_ref=got(o * 2 + core), send_sem=s_sem.at[i], recv_sem=r_sem.at[i],
                device_id=(sec, sibling), device_id_type=MESH))
        return copies

    def fill_g(o, to_ref):
        for q in range(slots):
            j, live = block(o, q)
            to_ref[q] = jnp.where(live, grad_ref[j], blank)

    def fill_s(held, o, to_ref):
        for q in range(slots):
            j, live = block(o, q)
            for m in range(2):
                to_ref[q, m] = jnp.where(live, held[j // 8, j % 8, m], blank)

    copies_g = sends(send_g, land_g.at[me], gs_sem, gr_sem)
    copies_a = sends(send_a, land_a.at[me], as_sem, ar_sem)
    copies_b = sends(send_b, got_b.at[me, every], bs_sem, br_sem)
    passes_g = forwards(lambda d: land_g.at[d], gfs_sem, gfr_sem)
    passes_a = forwards(lambda d: land_a.at[d], afs_sem, afr_sem)
    passes_b = forwards(lambda d: got_b.at[d, every], bfs_sem, bfr_sem)

    for o, cp in zip(chips + [chip], copies_g):
        fill_g(o, send_g.at[o])
        cp.start()
    fill_g(chip, land_g.at[me])

    for r in range(1, sections):
        pack((sec + r) % sections, 1, xsend.at[1, r])
    xcopies_b = xsends(1, xrecv_b)
    pack(sec, 0, xrecv_a.at[sec])
    pack(sec, 1, xrecv_b.at[sec])

    for cp in xcopies_a:
        cp.wait()
    for o, cp in zip(chips + [chip], copies_a):
        fill_s(xrecv_a, o, send_a.at[o])
        cp.start()
    fill_s(xrecv_a, chip, land_a.at[me])

    for cp in xcopies_b:
        cp.wait()
    for o in chips + [chip]:
        fill_s(xrecv_b, o, send_b.at[o])
    own_b = pltpu.make_async_copy(send_b.at[chip], got_b.at[me, every], out_sem.at[0])
    own_b.start()

    for cp, fw in zip(copies_g, passes_g):
        cp.wait_recv()
        fw.start()
    copies_g[-1].wait_recv()
    for fw in passes_g:
        fw.wait_recv()

    def flags(s):
        j, live = block(chip, 2 * s + core)
        return j % 4 < 2, live & (j % 2 == 0)

    for s in range(count):
        g = land_g[:, 2 * s + core].reshape(size)
        sums[s] = jnp.where(flags(s)[0], dotg(g, g, 1, 1), dotg(g, g, 0, 0))

    for i, (cp, fw) in enumerate(zip(copies_a, passes_a)):
        cp.wait_recv()
        fw.start()
        if i == 11:
            for other in copies_b:
                other.start()
    copies_a[-1].wait_recv()
    for fw in passes_a:
        fw.wait_recv()
    outs = [pltpu.make_async_copy(land_g, got_g.at[:, every], out_sem.at[1]),
            pltpu.make_async_copy(land_a, got_a.at[:, every], out_sem.at[2])]
    for cp in outs:
        cp.start()

    scale = (1.0 - ema_decay) / 512.0
    eye = (lax.broadcasted_iota(jnp.int32, size, 0) == lax.broadcasted_iota(jnp.int32, size, 1)).astype(f32)
    for s in range(count):
        q = 2 * s + core
        ema = split(ema_decay * land_a[:, q, 0].reshape(size).astype(f32) + scale * sums[s])
        old = land_a[:, q, 1].reshape(size)
        grown = dotg(ema[0], old, 1, 0) + dotg(ema[1], old, 1, 0)
        power[s] = grown
        ps = split(grown)
        cross[s] = jnp.where(flags(s)[1], dot3(ps, ps, 0, 0), eye)

    def share(p):
        part = pl.ds(0, count)
        return (pltpu.make_async_remote_copy(
            src_ref=fresh.at[p], dst_ref=got_f.at[core, p, part], send_sem=ffs_sem.at[p], recv_sem=ffr_sem.at[p],
            device_id=(sec, sibling), device_id_type=MESH),
            pltpu.make_async_copy(fresh.at[p], got_f.at[core, p, part], out_sem.at[3 + p]))

    def relay(p):
        for i in range(5 * p - 5, 5 * p):
            copies_b[i].wait_recv()
            passes_b[i].start()

    def step(p, _):
        factor_panel(p, cross, power, fresh, count)
        for cp in share(p):
            cp.start()
        for k in range(1, 4):
            pl.when(p == k)(functools.partial(relay, k))
        return 0
    lax.fori_loop(0, 4, step, 0)
    shared = [share(p)[0] for p in range(4)]
    outs += [share(p)[1] for p in range(4)]
    copies_b[-1].wait_recv()
    for cp in passes_b + shared:
        cp.wait_recv()
    own_b.wait()
    for cp in outs:
        cp.wait()
    for cp in copies_g + copies_a + copies_b + passes_g + passes_a + passes_b + shared:
        cp.wait_send()


def exchange(slots, group, table, grad, lg, rg, lb, rb):
    smem = pl.BlockSpec(memory_space=pltpu.SMEM)
    anym = pl.BlockSpec(memory_space=pl.ANY)
    dma = pltpu.SemaphoreType.DMA
    count = slots // 2
    return pl.pallas_call(
        functools.partial(exchange_kernel, slots),
        out_shape=[
            jax.ShapeDtypeStruct((32, CHIP, 16, 512), bf16),
            jax.ShapeDtypeStruct((32, CHIP, 2, 16, 512), bf16),
            jax.ShapeDtypeStruct((32, CHIP, 2, 16, 512), bf16),
            jax.ShapeDtypeStruct((2, 4, CHIP // 2, 512, 128), bf16),
        ],
        in_specs=[smem] * 2 + [anym] * 5,
        out_specs=[anym] * 4,
        scratch_shapes=[
            pltpu.VMEM((32, 16, 512), bf16),
            pltpu.VMEM((4, 32, 16, 512), f32),
            pltpu.VMEM((2, 4, 8, 2, 16, 512), bf16),
            pltpu.VMEM((4, 8, 2, 16, 512), bf16),
            pltpu.VMEM((4, 8, 2, 16, 512), bf16),
            pltpu.VMEM((CHIPS, slots, 16, 512), bf16),
            pltpu.VMEM((CHIPS, slots, 2, 16, 512), bf16),
            pltpu.VMEM((CHIPS, slots, 2, 16, 512), bf16),
            pltpu.VMEM((32, slots, 16, 512), bf16),
            pltpu.VMEM((32, slots, 2, 16, 512), bf16),
            pltpu.VMEM((count, 512, 512), f32),
            pltpu.VMEM((count, 512, 512), f32),
            pltpu.VMEM((count, 512, 512), f32),
            pltpu.VMEM((4, count, 512, 128), bf16),
            dma((5,)), dma((2, 4)), dma((2, 4)),
            dma((16,)), dma((16,)), dma((16,)), dma((16,)), dma((16,)), dma((16,)),
            dma((15,)), dma((15,)), dma((15,)), dma((15,)), dma((15,)), dma((15,)),
            dma((4,)), dma((4,)), dma((7,)),
        ],
        compiler_params=pltpu.CompilerParams(
            collective_id=slots, has_side_effects=True, vmem_limit_bytes=56 << 20),
    )(group, table, grad, lg, rg, lb, rb)


def finish_kernel(mine_ref, got_g, got_a, got_b, got_f,
                  out_lg, out_rg, out_lb, out_rb, out_rot,
                  g_in, a_in, b_in, f_in, ema, basis, turned, in_sem, out_sem):
    size = (512, 512)
    scale = (1.0 - ema_decay) / 512.0

    def slot(c):
        word = mine_ref[c]
        q = word // 64
        loads = [pltpu.make_async_copy(got_g.at[:, q], g_in.at[c], in_sem.at[c, 0]),
                 pltpu.make_async_copy(got_a.at[:, q], a_in.at[c], in_sem.at[c, 1]),
                 pltpu.make_async_copy(got_b.at[:, q], b_in.at[c], in_sem.at[c, 2]),
                 pltpu.make_async_copy(got_f.at[q % 2, :, q // 2], f_in.at[c], in_sem.at[c, 3])]
        return word % 64 - 1, word > 0, loads

    def put(c, kind, src, mine, other, flag):
        @pl.when(flag)
        def _():
            pltpu.make_async_copy(src, mine.at[c], out_sem.at[c, kind]).start()

        @pl.when(jnp.logical_not(flag))
        def _():
            pltpu.make_async_copy(src, other.at[c], out_sem.at[c, kind]).start()

    for c in range(CAP):
        _, live, loads = slot(c)

        @pl.when(live)
        def _():
            for cp in loads:
                cp.start()

    for c in range(CAP):
        j, live, loads = slot(c)

        @pl.when(live)
        def _():
            for cp in loads:
                cp.wait()
            is_left = j % 4 < 2
            basis[c, 1] = b_in[c, :, 1].reshape(size).astype(f32)
            put(c, 3, basis.at[c, 1], out_rb, out_lb, is_left)
            new = jnp.concatenate([f_in[c, p] for p in range(4)], axis=1)
            first = jnp.where(j % 2 == 0, new, a_in[c, :, 1].reshape(size))
            basis[c, 0] = first.astype(f32)
            put(c, 2, basis.at[c, 0], out_lb, out_rb, is_left)
            g = g_in[c].reshape(size)
            outer = dotg(g, g, 1, 1)
            inner = dotg(g, g, 0, 0)
            ema[c, 0] = (ema_decay * a_in[c, :, 0].reshape(size).astype(f32)
                         + scale * jnp.where(is_left, outer, inner))
            put(c, 0, ema.at[c, 0], out_lg, out_rg, is_left)
            ema[c, 1] = (ema_decay * b_in[c, :, 0].reshape(size).astype(f32)
                         + scale * jnp.where(is_left, inner, outer))
            put(c, 1, ema.at[c, 1], out_rg, out_lg, is_left)
            second = b_in[c, :, 1].reshape(size)
            low_left = jnp.where(is_left, first, second)
            low_right = jnp.where(is_left, second, first)
            half = dotg(low_left, g, 0, 0).astype(bf16)
            turned[c] = dotg(half, low_right, 1, 0).astype(bf16)
            pltpu.make_async_copy(turned.at[c], out_rot.at[c], out_sem.at[c, 4]).start()

        @pl.when(jnp.logical_not(live))
        def _():
            ema[c] = jnp.zeros((2,) + size, f32)
            turned[c] = jnp.zeros(size, bf16)
            for kind, out in enumerate((out_lg, out_rg, out_lb, out_rb)):
                pltpu.make_async_copy(ema.at[c, kind % 2], out.at[c], out_sem.at[c, kind]).start()
            pltpu.make_async_copy(turned.at[c], out_rot.at[c], out_sem.at[c, 4]).start()

    for c in range(CAP):
        for kind, out in enumerate((out_lg, out_rg, out_lb, out_rb)):
            pltpu.make_async_copy(ema.at[c, 0], out.at[c], out_sem.at[c, kind]).wait()
        pltpu.make_async_copy(turned.at[c], out_rot.at[c], out_sem.at[c, 4]).wait()


def finish(mine, got_g, got_a, got_b, got_f):
    smem = pl.BlockSpec(memory_space=pltpu.SMEM)
    anym = pl.BlockSpec(memory_space=pl.ANY)
    full = jax.ShapeDtypeStruct((CAP, 512, 512), f32)
    return pl.pallas_call(
        finish_kernel,
        out_shape=[full] * 4 + [jax.ShapeDtypeStruct((CAP, 512, 512), bf16)],
        in_specs=[smem] + [anym] * 4,
        out_specs=[anym] * 5,
        scratch_shapes=[
            pltpu.VMEM((CAP, 32, 16, 512), bf16),
            pltpu.VMEM((CAP, 32, 2, 16, 512), bf16),
            pltpu.VMEM((CAP, 32, 2, 16, 512), bf16),
            pltpu.VMEM((CAP, 4, 512, 128), bf16),
            pltpu.VMEM((CAP, 2, 512, 512), f32),
            pltpu.VMEM((CAP, 2, 512, 512), f32),
            pltpu.VMEM((CAP, 512, 512), bf16),
            pltpu.SemaphoreType.DMA((CAP, 4)),
            pltpu.SemaphoreType.DMA((CAP, 5)),
        ],
        compiler_params=pltpu.CompilerParams(vmem_limit_bytes=56 << 20),
    )(mine, got_g, got_a, got_b, got_f)


def shards(gradient, left_gram, right_gram, left_basis, right_basis, migration, owners):
    sections = lax.axis_size("section")
    blocks = gradient.shape[1]
    here_section = lax.axis_index("section")
    here_member = lax.axis_index("dp")
    own_row = lax.dynamic_index_in_dim(migration, here_section, 0, keepdims=False)
    targets = jnp.arange(sections, dtype=jnp.int32)
    send_group = jnp.sum(jnp.where(own_row[None, :] == targets[:, None], targets[None, :], 0), axis=1)

    listed = owners[:, :, 0]
    chip = listed // 2
    positions = jnp.arange(blocks, dtype=jnp.int32)
    before = positions[None, :] < positions[:, None]
    rank = jnp.sum(((listed[:, None, :] == listed[:, :, None]) & before).astype(jnp.int32), axis=2)
    chip_rank = jnp.sum(((chip[:, None, :] == chip[:, :, None]) & before).astype(jnp.int32), axis=2)
    few = jnp.max(chip_rank) < 4

    def here(x):
        return lax.dynamic_index_in_dim(x, here_section, 0, keepdims=False)
    place = here(chip * CHIP + chip_rank)
    slot = here(jnp.where(listed == here_member, rank, CAP))
    word = positions + 1 + 64 * here(chip_rank)
    table = jnp.sum(jnp.where(place[None, :] == jnp.arange(CHIPS * CHIP)[:, None], word[None, :], 0), axis=1)
    mine = jnp.sum(jnp.where(slot[None, :] == jnp.arange(CAP)[:, None], word[None, :], 0), axis=1)

    got = lax.cond(few, functools.partial(exchange, 4), functools.partial(exchange, CHIP),
                   send_group, table, gradient[0], left_gram[0], right_gram[0], left_basis[0], right_basis[0])
    outs = finish(mine, *got)
    return tuple(o[None] for o in outs)


def solution(mesh):
    in_specs = (P("section", None, "dp", None),) * 5 + (P(), P())
    out_specs = (P("section", "dp", None, None),) * 5
    return jax.shard_map(shards, mesh=mesh, in_specs=in_specs, out_specs=out_specs, check_vma=False)
```

```python
import functools

import jax
import jax.numpy as jnp
from jax import lax
from jax.experimental import pallas as pl
from jax.experimental.pallas import tpu as pltpu
from jax.sharding import PartitionSpec as P

CAP = 3
MESH = pl.DeviceIdType.MESH
bf16, f32 = jnp.bfloat16, jnp.float32
ema_decay = 0.9


def dotg(a, b, ca, cb):
    return lax.dot_general(a, b, (((ca,), (cb,)), ((), ())), preferred_element_type=f32)


def split(x):
    high = x.astype(bf16)
    return high, (x - high.astype(f32)).astype(bf16)


def dot3(a, b, ca, cb):
    return dotg(jnp.concatenate([a[0], a[0], a[1]], axis=ca), jnp.concatenate([b[0], b[1], b[0]], axis=cb), ca, cb)


def eliminate(mats, base, m):
    sub = lax.broadcasted_iota(jnp.int32, (8, 128), 0)
    row = lax.broadcasted_iota(jnp.int32, (64, 128), 0)
    lane = lax.broadcasted_iota(jnp.int32, (64, 128), 1)
    left = list(mats)
    done = [[] for _ in mats]
    for k in range(0, 64, m):
        o = k % 8
        for s in range(len(mats)):
            a = left[s]
            n = a.shape[0]
            at = base + k
            b = [jnp.broadcast_to(a[:, at + i:at + i + 1], (n, 128)) for i in range(m)]
            ra = [a[o + i:o + i + 1, :] for i in range(m)]
            c = [[b[i][o + q:o + q + 1, :] for i in range(m)] for q in range(m)]
            inv = []
            for i in range(m):
                inv.append(1.0 / c[i][i])
                for q in range(i + 1, m):
                    l = c[q][i] * inv[i]
                    ra[q] = ra[q] - l * ra[i]
                    for j in range(i + 1, m):
                        c[q][j] = c[q][j] - l * c[i][j]
            f = []
            for i in range(m):
                x = b[i]
                for q in range(i):
                    x = x - f[q] * c[q][i]
                x = x * inv[i]
                top = jnp.where(sub > o + i, x[:8], 0.0)
                f.append(top if n == 8 else jnp.concatenate([top, x[8:]], axis=0))
            for i in range(m):
                a = a - f[i] * ra[i]
            if o + m == 8:
                done[s].append(a[:8])
                a = a[8:]
            left[s] = a
    keep = (lane < 64) if base == 0 else (lane >= 64)
    out = []
    for s in range(len(mats)):
        a = jnp.concatenate(done[s], axis=0)
        d = jnp.sum(jnp.where(lane == row + base, a, 0.0), axis=1, keepdims=True)
        out.append(jnp.where(keep, pltpu.roll(a * lax.rsqrt(d), 64, 1), 0.0))
    return out


def inv_chol(mats, m=4):
    row = lax.broadcasted_iota(jnp.int32, (64, 128), 0)
    lane = lax.broadcasted_iota(jnp.int32, (64, 128), 1)
    low = lane < 64
    m1 = eliminate([jnp.where(low, d[:64], jnp.where(lane == row + 64, 1.0, 0.0)) for d in mats], 0, m)
    m1s = [split(x) for x in m1]
    zero = jnp.zeros((64, 128), f32)
    u, second = [], []
    for s, d in enumerate(mats):
        right = jnp.concatenate([jnp.where(low, 0.0, d[:64]), zero], axis=0)
        u.append(split(dot3(m1s[s], split(right), 1, 0)))
        rest = d[64:] - dot3(u[s], u[s], 0, 0)[64:]
        second.append(jnp.where(low, jnp.where(lane == row, 1.0, 0.0), rest))
    mixed = [split(dot3(u[s], m1s[s], 0, 0)) for s in range(len(mats))]
    m2 = eliminate(second, 64, m)
    return [jnp.concatenate([m1[s], m2[s] - dot3(split(m2[s]), mixed[s], 1, 0)], axis=0)
            for s in range(len(mats))]


def factor_panel(p, cross, power, fresh, count):
    at = pl.ds(pl.multiple_of(p * 128, 128), 128)
    inv = [split(x) for x in inv_chol([cross[s, at, at] for s in range(count)])]
    new = [dot3(split(power[s, :, at]), inv[s], 1, 1) for s in range(count)]
    for s in range(count):
        fresh[p, s] = new[s].astype(bf16)

    def rest(lo, hi):
        u = [split(dot3(inv[s], split(cross[s, lo:hi, hi:]), 1, 0)) for s in range(count)]
        for s in range(count):
            cross[s, hi:, hi:] = cross[s, hi:, hi:] - dot3(u[s], u[s], 0, 0)
            power[s, :, hi:] = power[s, :, hi:] - dot3(split(new[s]), u[s], 1, 0)

    for k in range(3):
        pl.when(p == k)(functools.partial(rest, 128 * k, 128 * k + 128))


def whole_gram(rows):
    part = [rows[128 * i:128 * i + 128, :384].astype(f32) for i in range(4)]
    lines = []
    for i in range(4):
        line = []
        for j in range(4):
            t = (j - i) % 4
            line.append(part[j][:, 128:256].T if t == 3 else part[i][:, 128 * t:128 * t + 128])
        lines.append(jnp.concatenate(line, axis=1))
    return jnp.concatenate(lines, axis=0)


CHIP = 6
CHIPS = 16
WIDE = 896
FAR_FIRST = [(2, 2), (1, 2), (3, 2), (2, 1), (2, 3), (1, 1), (3, 3), (1, 3), (3, 1), (0, 2), (2, 0),
             (0, 1), (1, 0), (0, 3), (3, 0)]


def exchange_kernel(slots, moves_ref, table_ref, grad_hbm, lg_hbm, rg_hbm, lb_hbm, rb_hbm,
                    got_g, got_a, got_b, got_f,
                    grad_ref, state, xsend, xrecv_a, xrecv_b, send_g, send_a, send_b,
                    land_g, land_a, sums, cross, power, fresh,
                    in_sem, xs_sem, xr_sem, gs_sem, gr_sem, as_sem, ar_sem, bs_sem, br_sem,
                    gfs_sem, gfr_sem, afs_sem, afr_sem, bfs_sem, bfr_sem, ffs_sem, ffr_sem, out_sem):
    sec = lax.axis_index("section")
    me = lax.axis_index("dp")
    sections = 4
    count = slots // 2
    core, z, y = me % 2, (me // 2) % 4, me // 8
    chip = me // 2
    sibling = chip * 2 + 1 - core
    chips = [((y + off[0]) % 4) * 4 + (z + off[1]) % 4 for off in FAR_FIRST]
    back = [((y + 4 - off[0]) % 4) * 4 + (z + 4 - off[1]) % 4 for off in FAR_FIRST]
    size = (512, 512)
    blank = jnp.zeros((16, 512), bf16)
    blank_wide = jnp.zeros((16, WIDE), bf16)
    every = pl.ds(0, slots)

    fetches = [pltpu.make_async_copy(grad_hbm, grad_ref, in_sem.at[4])]
    fetches += [pltpu.make_async_copy(src, state.at[i], in_sem.at[i])
                for i, src in enumerate((lg_hbm, lb_hbm, rg_hbm, rb_hbm))]
    for cp in fetches:
        cp.start()

    barrier = pltpu.get_barrier_semaphore()
    for r in range(1, sections):
        pl.semaphore_signal(barrier, inc=1, device_id=((sec + r) % sections, me), device_id_type=MESH)
    pl.semaphore_signal(barrier, inc=1, device_id=(sec, sibling), device_id_type=MESH)
    for o in chips:
        pl.semaphore_signal(barrier, inc=1, device_id=(sec, o * 2 + core), device_id_type=MESH)

    def pack(target, half, to_ref):
        base = functools.reduce(
            jnp.maximum, [jnp.where(moves_ref[sec, g] == target, g * 8, 0) for g in range(sections)])
        for k in range(8):
            side = (k % 4 >= 2) != (half == 1)
            for t in range(3):
                at = pl.ds(pl.multiple_of(((y + t) % 4) * 128, 128), 128)
                to_ref[k, :, 128 * t:128 * t + 128] = state[2 * side, base + k, :, at].astype(bf16)
            to_ref[k, :, 384:] = state[2 * side + 1, base + k].astype(bf16)

    def xsends(half, landing):
        copies = []
        for r in (2, 1, 3):
            t = (sec + r) % sections
            copies.append(pltpu.make_async_remote_copy(
                src_ref=xsend.at[half, r], dst_ref=landing.at[sec],
                send_sem=xs_sem.at[half, r], recv_sem=xr_sem.at[half, r],
                device_id=(t, me), device_id_type=MESH))
            copies[-1].start()
        return copies

    def block(o, q):
        j = table_ref[o * CHIP + q] % 64 - 1
        return jnp.maximum(j, 0), j >= 0

    def sends(ref, got, s_sem, r_sem, part=every):
        copies = []
        for i, (o, c) in enumerate([(o, core) for o in chips] + [(chip, 1 - core)]):
            copies.append(pltpu.make_async_remote_copy(
                src_ref=ref.at[o, part], dst_ref=got.at[me, part], send_sem=s_sem.at[i], recv_sem=r_sem.at[i],
                device_id=(sec, o * 2 + c), device_id_type=MESH))
        return copies

    def forwards(got, s_sem, r_sem, part=every):
        copies = []
        for i, o in enumerate(back):
            copies.append(pltpu.make_async_remote_copy(
                src_ref=got.at[o * 2 + core, part], dst_ref=got.at[o * 2 + core, part],
                send_sem=s_sem.at[i], recv_sem=r_sem.at[i],
                device_id=(sec, sibling), device_id_type=MESH))
        return copies

    def fill_g(o, to_ref):
        for q in range(slots):
            j, live = block(o, q)
            to_ref[q] = jnp.where(live, grad_ref[j], blank)

    def fill_s(held, o, to_ref, first=0, last=slots):
        for q in range(first, last):
            j, live = block(o, q)
            to_ref[q] = jnp.where(live, held[j // 8, j % 8], blank_wide)

    pairs = [pl.ds(2 * s, 2) for s in range(count)]
    copies_g = sends(send_g, land_g, gs_sem, gr_sem)
    copies_a = [sends(send_a, land_a, as_sem.at[s], ar_sem.at[s], pairs[s]) for s in range(count)]
    copies_b = sends(send_b, got_b, bs_sem, br_sem)
    passes_g = forwards(land_g, gfs_sem, gfr_sem)
    passes_a = [forwards(land_a, afs_sem.at[s], afr_sem.at[s], pairs[s]) for s in range(count)]
    passes_b = forwards(got_b, bfs_sem, bfr_sem)

    fetches[0].wait()
    def each_chip(fill):
        def one(o, _):
            fill(o)
            return 0
        lax.fori_loop(0, CHIPS, one, 0)

    def each_section(half):
        def one(r, _):
            pack((sec + r) % sections, half, xsend.at[half, r])
            return 0
        lax.fori_loop(1, sections, one, 0)

    each_chip(lambda o: fill_g(o, send_g.at[o]))
    land_g[me] = send_g[chip]
    for cp in fetches[1:]:
        cp.wait()
    each_section(0)
    pl.semaphore_wait(barrier, sections - 1 + 1 + len(chips))
    xcopies_a = xsends(0, xrecv_a)
    for cp in copies_g:
        cp.start()

    each_section(1)
    xcopies_b = xsends(1, xrecv_b)
    pack(sec, 0, xrecv_a.at[sec])
    pack(sec, 1, xrecv_b.at[sec])

    for cp in xcopies_a:
        cp.wait()
    for s in range(count):
        each_chip(lambda o: fill_s(xrecv_a, o, send_a.at[o], 2 * s, 2 * s + 2))
        for cp in copies_a[s]:
            cp.start()
    land_a[me] = send_a[chip]

    for cp in xcopies_b:
        cp.wait()
    each_chip(lambda o: fill_s(xrecv_b, o, send_b.at[o]))
    own_b = pltpu.make_async_copy(send_b.at[chip], got_b.at[me, every], out_sem.at[0])
    own_b.start()

    for cp, fw in zip(copies_g, passes_g):
        cp.wait_recv()
        fw.start()
    copies_g[-1].wait_recv()
    for fw in passes_g:
        fw.wait_recv()

    def flags(s):
        j, live = block(chip, 2 * s + core)
        return j % 4 < 2, live & (j % 2 == 0)

    for s in range(count):
        g = land_g[:, 2 * s + core].reshape(size)
        sums[s] = jnp.where(flags(s)[0], dotg(g, g, 1, 1), dotg(g, g, 0, 0))

    scale = (1.0 - ema_decay) / 512.0
    eye = (lax.broadcasted_iota(jnp.int32, size, 0) == lax.broadcasted_iota(jnp.int32, size, 1)).astype(f32)
    for s in range(count):
        for i, (cp, fw) in enumerate(zip(copies_a[s], passes_a[s])):
            cp.wait_recv()
            fw.start()
            if s == count - 1 and i == 9:
                for other in copies_b:
                    other.start()
        copies_a[s][-1].wait_recv()
        for fw in passes_a[s]:
            fw.wait_recv()
        q = 2 * s + core
        ema = split(ema_decay * whole_gram(land_a[:, q].reshape(512, WIDE)) + scale * sums[s])
        old = land_a[:, q, :, 384:].reshape(size)
        grown = dotg(ema[0], old, 1, 0) + dotg(ema[1], old, 1, 0)
        power[s] = grown
        ps = split(grown)
        cross[s] = jnp.where(flags(s)[1], dot3(ps, ps, 0, 0), eye)
    outs = [pltpu.make_async_copy(land_g, got_g.at[:, every], out_sem.at[1]),
            pltpu.make_async_copy(land_a, got_a.at[:, every], out_sem.at[2])]
    for cp in outs:
        cp.start()

    def share(p):
        part = pl.ds(0, count)
        return (pltpu.make_async_remote_copy(
            src_ref=fresh.at[p], dst_ref=got_f.at[core, p, part], send_sem=ffs_sem.at[p], recv_sem=ffr_sem.at[p],
            device_id=(sec, sibling), device_id_type=MESH),
            pltpu.make_async_copy(fresh.at[p], got_f.at[core, p, part], out_sem.at[3 + p]))

    def relay(p):
        for i in range(5 * p - 5, 5 * p):
            copies_b[i].wait_recv()
            passes_b[i].start()

    def step(p, _):
        factor_panel(p, cross, power, fresh, count)
        for cp in share(p):
            cp.start()
        for k in range(1, 4):
            pl.when(p == k)(functools.partial(relay, k))
        return 0
    lax.fori_loop(0, 4, step, 0)
    shared = [share(p)[0] for p in range(4)]
    outs += [share(p)[1] for p in range(4)]
    copies_b[-1].wait_recv()
    for cp in passes_b + shared:
        cp.wait_recv()
    own_b.wait()
    for cp in outs:
        cp.wait()
    for cp in copies_g + sum(copies_a, []) + copies_b + passes_g + sum(passes_a, []) + passes_b + shared:
        cp.wait_send()


def exchange(slots, moves, table, grad, lg, rg, lb, rb):
    smem = pl.BlockSpec(memory_space=pltpu.SMEM)
    anym = pl.BlockSpec(memory_space=pl.ANY)
    dma = pltpu.SemaphoreType.DMA
    count = slots // 2
    return pl.pallas_call(
        functools.partial(exchange_kernel, slots),
        out_shape=[
            jax.ShapeDtypeStruct((32, CHIP, 16, 512), bf16),
            jax.ShapeDtypeStruct((32, CHIP, 16, WIDE), bf16),
            jax.ShapeDtypeStruct((32, CHIP, 16, WIDE), bf16),
            jax.ShapeDtypeStruct((2, 4, CHIP // 2, 512, 128), bf16),
        ],
        in_specs=[smem] * 2 + [anym] * 5,
        out_specs=[anym] * 4,
        scratch_shapes=[
            pltpu.VMEM((32, 16, 512), bf16),
            pltpu.VMEM((4, 32, 16, 512), f32),
            pltpu.VMEM((2, 4, 8, 16, WIDE), bf16),
            pltpu.VMEM((4, 8, 16, WIDE), bf16),
            pltpu.VMEM((4, 8, 16, WIDE), bf16),
            pltpu.VMEM((CHIPS, slots, 16, 512), bf16),
            pltpu.VMEM((CHIPS, slots, 16, WIDE), bf16),
            pltpu.VMEM((CHIPS, slots, 16, WIDE), bf16),
            pltpu.VMEM((32, slots, 16, 512), bf16),
            pltpu.VMEM((32, slots, 16, WIDE), bf16),
            pltpu.VMEM((count, 512, 512), f32),
            pltpu.VMEM((count, 512, 512), f32),
            pltpu.VMEM((count, 512, 512), f32),
            pltpu.VMEM((4, count, 512, 128), bf16),
            dma((5,)), dma((2, 4)), dma((2, 4)),
            dma((16,)), dma((16,)), dma((count, 16)), dma((count, 16)), dma((16,)), dma((16,)),
            dma((15,)), dma((15,)), dma((count, 15)), dma((count, 15)), dma((15,)), dma((15,)),
            dma((4,)), dma((4,)), dma((7,)),
        ],
        compiler_params=pltpu.CompilerParams(
            collective_id=slots, has_side_effects=True, vmem_limit_bytes=40 << 20),
    )(moves, table, grad, lg, rg, lb, rb)


def finish_kernel(table_ref, got_g, got_a, got_b, got_f,
                  out_lg, out_rg, out_lb, out_rb, out_rot,
                  g_in, a_in, b_in, f_in, ema, basis, turned, in_sem, out_sem):
    size = (512, 512)
    scale = (1.0 - ema_decay) / 512.0

    def slot(c):
        word = table_ref[CHIPS * CHIP + c]
        q = word // 64
        loads = [pltpu.make_async_copy(got_g.at[:, q], g_in.at[c], in_sem.at[c, 0]),
                 pltpu.make_async_copy(got_a.at[:, q], a_in.at[c], in_sem.at[c, 1]),
                 pltpu.make_async_copy(got_b.at[:, q], b_in.at[c], in_sem.at[c, 2]),
                 pltpu.make_async_copy(got_f.at[q % 2, :, q // 2], f_in.at[c], in_sem.at[c, 3])]
        return word % 64 - 1, word > 0, loads

    def put(c, kind, src, mine, other, flag):
        @pl.when(flag)
        def _():
            pltpu.make_async_copy(src, mine.at[c], out_sem.at[c, kind]).start()

        @pl.when(jnp.logical_not(flag))
        def _():
            pltpu.make_async_copy(src, other.at[c], out_sem.at[c, kind]).start()

    for c in range(CAP):
        _, live, loads = slot(c)

        @pl.when(live)
        def _():
            for cp in loads:
                cp.start()

    for c in range(CAP):
        j, live, loads = slot(c)

        @pl.when(live)
        def _():
            for cp in loads:
                cp.wait()
            is_left = j % 4 < 2
            second = b_in[c, :, :, 384:].reshape(size)
            basis[c, 1] = second.astype(f32)
            put(c, 3, basis.at[c, 1], out_rb, out_lb, is_left)
            new = jnp.concatenate([f_in[c, p] for p in range(4)], axis=1)
            first = jnp.where(j % 2 == 0, new, a_in[c, :, :, 384:].reshape(size))
            basis[c, 0] = first.astype(f32)
            put(c, 2, basis.at[c, 0], out_lb, out_rb, is_left)
            g = g_in[c].reshape(size)
            outer = dotg(g, g, 1, 1)
            inner = dotg(g, g, 0, 0)
            ema[c, 0] = (ema_decay * whole_gram(a_in[c].reshape(512, WIDE))
                         + scale * jnp.where(is_left, outer, inner))
            put(c, 0, ema.at[c, 0], out_lg, out_rg, is_left)
            ema[c, 1] = (ema_decay * whole_gram(b_in[c].reshape(512, WIDE))
                         + scale * jnp.where(is_left, inner, outer))
            put(c, 1, ema.at[c, 1], out_rg, out_lg, is_left)
            low_left = jnp.where(is_left, first, second)
            low_right = jnp.where(is_left, second, first)
            half = dotg(low_left, g, 0, 0).astype(bf16)
            turned[c] = dotg(half, low_right, 1, 0).astype(bf16)
            pltpu.make_async_copy(turned.at[c], out_rot.at[c], out_sem.at[c, 4]).start()

        @pl.when(jnp.logical_not(live))
        def _():
            ema[c] = jnp.zeros((2,) + size, f32)
            turned[c] = jnp.zeros(size, bf16)
            for kind, out in enumerate((out_lg, out_rg, out_lb, out_rb)):
                pltpu.make_async_copy(ema.at[c, kind % 2], out.at[c], out_sem.at[c, kind]).start()
            pltpu.make_async_copy(turned.at[c], out_rot.at[c], out_sem.at[c, 4]).start()

    for c in range(CAP):
        for kind, out in enumerate((out_lg, out_rg, out_lb, out_rb)):
            pltpu.make_async_copy(ema.at[c, 0], out.at[c], out_sem.at[c, kind]).wait()
        pltpu.make_async_copy(turned.at[c], out_rot.at[c], out_sem.at[c, 4]).wait()


def finish(table, got_g, got_a, got_b, got_f):
    smem = pl.BlockSpec(memory_space=pltpu.SMEM)
    anym = pl.BlockSpec(memory_space=pl.ANY)
    full = jax.ShapeDtypeStruct((CAP, 512, 512), f32)
    return pl.pallas_call(
        finish_kernel,
        out_shape=[full] * 4 + [jax.ShapeDtypeStruct((CAP, 512, 512), bf16)],
        in_specs=[smem] + [anym] * 4,
        out_specs=[anym] * 5,
        scratch_shapes=[
            pltpu.VMEM((CAP, 32, 16, 512), bf16),
            pltpu.VMEM((CAP, 32, 16, WIDE), bf16),
            pltpu.VMEM((CAP, 32, 16, WIDE), bf16),
            pltpu.VMEM((CAP, 4, 512, 128), bf16),
            pltpu.VMEM((CAP, 2, 512, 512), f32),
            pltpu.VMEM((CAP, 2, 512, 512), f32),
            pltpu.VMEM((CAP, 512, 512), bf16),
            pltpu.SemaphoreType.DMA((CAP, 4)),
            pltpu.SemaphoreType.DMA((CAP, 5)),
        ],
        compiler_params=pltpu.CompilerParams(vmem_limit_bytes=28 << 20),
    )(table, got_g, got_a, got_b, got_f)


def shards(gradient, left_gram, right_gram, left_basis, right_basis, migration, owners):
    sections = lax.axis_size("section")
    blocks = gradient.shape[1]
    here_section = lax.axis_index("section")
    here_member = lax.axis_index("dp")
    listed = owners[:, :, 0]
    chip = lax.shift_right_logical(listed, 1)
    positions = jnp.arange(blocks, dtype=jnp.int32)
    before = positions[None, :] < positions[:, None]
    rank = jnp.sum(((listed[:, None, :] == listed[:, :, None]) & before).astype(jnp.int32), axis=2)
    chip_rank = jnp.sum(((chip[:, None, :] == chip[:, :, None]) & before).astype(jnp.int32), axis=2)
    few = jnp.max(chip_rank) < 4

    local = jnp.arange(sections, dtype=jnp.int32)[:, None] == here_section
    word = positions[None, :] + 1 + 64 * chip_rank
    place = jnp.where(local, chip * CHIP + chip_rank, -1)
    own = jnp.where(local & (listed == here_member), CHIPS * CHIP + rank, -1)
    entry = jnp.arange(CHIPS * CHIP + CAP, dtype=jnp.int32)[:, None, None]
    table = jnp.sum(jnp.where((place[None] == entry) | (own[None] == entry), word[None], 0), axis=(1, 2))

    got = lax.cond(few, functools.partial(exchange, 4), functools.partial(exchange, CHIP),
                   migration, table, gradient[0], left_gram[0], right_gram[0], left_basis[0], right_basis[0])
    outs = finish(table, *got)
    return tuple(o[None] for o in outs)


def solution(mesh):
    in_specs = (P("section", None, "dp", None),) * 5 + (P(), P())
    out_specs = (P("section", "dp", None, None),) * 5
    return jax.shard_map(shards, mesh=mesh, in_specs=in_specs, out_specs=out_specs, check_vma=False)
```

```python
import functools

import jax
import jax.numpy as jnp
from jax import lax
from jax.experimental import pallas as pl
from jax.experimental.pallas import tpu as pltpu
from jax.sharding import PartitionSpec as P

CAP = 3
MESH = pl.DeviceIdType.MESH
bf16, f32 = jnp.bfloat16, jnp.float32
ema_decay = 0.9


def dotg(a, b, ca, cb):
    return lax.dot_general(a, b, (((ca,), (cb,)), ((), ())), preferred_element_type=f32)


def split(x):
    high = x.astype(bf16)
    return high, (x - high.astype(f32)).astype(bf16)


def dot3(a, b, ca, cb):
    return dotg(jnp.concatenate([a[0], a[0], a[1]], axis=ca), jnp.concatenate([b[0], b[1], b[0]], axis=cb), ca, cb)


def eliminate(mats, base, m):
    sub = lax.broadcasted_iota(jnp.int32, (8, 128), 0)
    row = lax.broadcasted_iota(jnp.int32, (64, 128), 0)
    lane = lax.broadcasted_iota(jnp.int32, (64, 128), 1)
    left = list(mats)
    done = [[] for _ in mats]
    for k in range(0, 64, m):
        o = k % 8
        for s in range(len(mats)):
            a = left[s]
            n = a.shape[0]
            at = base + k
            b = [jnp.broadcast_to(a[:, at + i:at + i + 1], (n, 128)) for i in range(m)]
            ra = [a[o + i:o + i + 1, :] for i in range(m)]
            c = [[b[i][o + q:o + q + 1, :] for i in range(m)] for q in range(m)]
            inv = []
            for i in range(m):
                inv.append(1.0 / c[i][i])
                for q in range(i + 1, m):
                    l = c[q][i] * inv[i]
                    ra[q] = ra[q] - l * ra[i]
                    for j in range(i + 1, m):
                        c[q][j] = c[q][j] - l * c[i][j]
            f = []
            for i in range(m):
                x = b[i]
                for q in range(i):
                    x = x - f[q] * c[q][i]
                x = x * inv[i]
                top = jnp.where(sub > o + i, x[:8], 0.0)
                f.append(top if n == 8 else jnp.concatenate([top, x[8:]], axis=0))
            for i in range(m):
                a = a - f[i] * ra[i]
            if o + m == 8:
                done[s].append(a[:8])
                a = a[8:]
            left[s] = a
    keep = (lane < 64) if base == 0 else (lane >= 64)
    out = []
    for s in range(len(mats)):
        a = jnp.concatenate(done[s], axis=0)
        d = jnp.sum(jnp.where(lane == row + base, a, 0.0), axis=1, keepdims=True)
        out.append(jnp.where(keep, pltpu.roll(a * lax.rsqrt(d), 64, 1), 0.0))
    return out


def inv_chol(mats, m=4):
    row = lax.broadcasted_iota(jnp.int32, (64, 128), 0)
    lane = lax.broadcasted_iota(jnp.int32, (64, 128), 1)
    low = lane < 64
    m1 = eliminate([jnp.where(low, d[:64], jnp.where(lane == row + 64, 1.0, 0.0)) for d in mats], 0, m)
    m1s = [split(x) for x in m1]
    zero = jnp.zeros((64, 128), f32)
    u, second = [], []
    for s, d in enumerate(mats):
        right = jnp.concatenate([jnp.where(low, 0.0, d[:64]), zero], axis=0)
        u.append(split(dot3(m1s[s], split(right), 1, 0)))
        rest = d[64:] - dot3(u[s], u[s], 0, 0)[64:]
        second.append(jnp.where(low, jnp.where(lane == row, 1.0, 0.0), rest))
    mixed = [split(dot3(u[s], m1s[s], 0, 0)) for s in range(len(mats))]
    m2 = eliminate(second, 64, m)
    return [jnp.concatenate([m1[s], m2[s] - dot3(split(m2[s]), mixed[s], 1, 0)], axis=0)
            for s in range(len(mats))]


def factor_panel(p, cross, power, fresh, count):
    at = pl.ds(pl.multiple_of(p * 128, 128), 128)
    inv = [split(x) for x in inv_chol([cross[s, at, at] for s in range(count)])]
    new = [dot3(split(power[s, :, at]), inv[s], 1, 1) for s in range(count)]
    for s in range(count):
        fresh[p, s] = new[s].astype(bf16)

    def rest(lo, hi):
        u = [split(dot3(inv[s], split(cross[s, lo:hi, hi:]), 1, 0)) for s in range(count)]
        for s in range(count):
            cross[s, hi:, hi:] = cross[s, hi:, hi:] - dot3(u[s], u[s], 0, 0)
            power[s, :, hi:] = power[s, :, hi:] - dot3(split(new[s]), u[s], 1, 0)

    for k in range(3):
        pl.when(p == k)(functools.partial(rest, 128 * k, 128 * k + 128))


def whole_gram(rows):
    part = [rows[128 * i:128 * i + 128, :384].astype(f32) for i in range(4)]
    lines = []
    for i in range(4):
        line = []
        for j in range(4):
            t = (j - i) % 4
            line.append(part[j][:, 128:256].T if t == 3 else part[i][:, 128 * t:128 * t + 128])
        lines.append(jnp.concatenate(line, axis=1))
    return jnp.concatenate(lines, axis=0)


CHIP = 6
CHIPS = 16
WIDE = 896
FAR_FIRST = [(2, 2), (1, 2), (3, 2), (2, 1), (2, 3), (1, 1), (3, 3), (1, 3), (3, 1), (0, 2), (2, 0),
             (0, 1), (1, 0), (0, 3), (3, 0)]


def exchange_kernel(slots, moves_ref, table_ref, grad_hbm, lg_hbm, rg_hbm, lb_hbm, rb_hbm,
                    got_g, got_a, got_b, got_f,
                    grad_ref, state, xsend, xrecv_a, xrecv_b, send_g, send_a, send_b,
                    land_g, land_a, sums, cross, power, fresh,
                    in_sem, xs_sem, xr_sem, gs_sem, gr_sem, as_sem, ar_sem, bs_sem, br_sem,
                    gfs_sem, gfr_sem, afs_sem, afr_sem, bfs_sem, bfr_sem, ffs_sem, ffr_sem, out_sem):
    sec = lax.axis_index("section")
    me = lax.axis_index("dp")
    sections = 4
    count = slots // 2
    core, z, y = me % 2, (me // 2) % 4, me // 8
    chip = me // 2
    sibling = chip * 2 + 1 - core
    chips = [((y + off[0]) % 4) * 4 + (z + off[1]) % 4 for off in FAR_FIRST]
    back = [((y + 4 - off[0]) % 4) * 4 + (z + 4 - off[1]) % 4 for off in FAR_FIRST]
    size = (512, 512)
    blank = jnp.zeros((16, 512), bf16)
    blank_wide = jnp.zeros((16, WIDE), bf16)
    every = pl.ds(0, slots)

    fetches = [pltpu.make_async_copy(grad_hbm, grad_ref, in_sem.at[4])]
    fetches += [pltpu.make_async_copy(src, state.at[i], in_sem.at[i])
                for i, src in enumerate((lg_hbm, lb_hbm, rg_hbm, rb_hbm))]
    for cp in fetches:
        cp.start()

    barrier = pltpu.get_barrier_semaphore()
    for r in range(1, sections):
        pl.semaphore_signal(barrier, inc=1, device_id=((sec + r) % sections, me), device_id_type=MESH)
    pl.semaphore_signal(barrier, inc=1, device_id=(sec, sibling), device_id_type=MESH)
    for o in chips:
        pl.semaphore_signal(barrier, inc=1, device_id=(sec, o * 2 + core), device_id_type=MESH)

    def pack(target, half, to_ref):
        base = functools.reduce(
            jnp.maximum, [jnp.where(moves_ref[sec, g] == target, g * 8, 0) for g in range(sections)])
        for k in range(8):
            side = (k % 4 >= 2) != (half == 1)
            for t in range(3):
                at = pl.ds(pl.multiple_of(((y + t) % 4) * 128, 128), 128)
                to_ref[k, :, 128 * t:128 * t + 128] = state[2 * side, base + k, :, at].astype(bf16)
            to_ref[k, :, 384:] = state[2 * side + 1, base + k].astype(bf16)

    def xsends(half, landing):
        copies = []
        for r in (2, 1, 3):
            t = (sec + r) % sections
            copies.append(pltpu.make_async_remote_copy(
                src_ref=xsend.at[half, r], dst_ref=landing.at[sec],
                send_sem=xs_sem.at[half, r], recv_sem=xr_sem.at[half, r],
                device_id=(t, me), device_id_type=MESH))
            copies[-1].start()
        return copies

    def block(o, q):
        j = table_ref[o * CHIP + q] % 64 - 1
        return jnp.maximum(j, 0), j >= 0

    def sends(ref, got, s_sem, r_sem, part=every):
        copies = []
        for i, (o, c) in enumerate([(o, core) for o in chips] + [(chip, 1 - core)]):
            copies.append(pltpu.make_async_remote_copy(
                src_ref=ref.at[o, part], dst_ref=got.at[me, part], send_sem=s_sem.at[i], recv_sem=r_sem.at[i],
                device_id=(sec, o * 2 + c), device_id_type=MESH))
        return copies

    def forwards(got, s_sem, r_sem, part=every):
        copies = []
        for i, o in enumerate(back):
            copies.append(pltpu.make_async_remote_copy(
                src_ref=got.at[o * 2 + core, part], dst_ref=got.at[o * 2 + core, part],
                send_sem=s_sem.at[i], recv_sem=r_sem.at[i],
                device_id=(sec, sibling), device_id_type=MESH))
        return copies

    def fill_g(o, to_ref):
        for q in range(slots):
            j, live = block(o, q)
            to_ref[q] = jnp.where(live, grad_ref[j], blank)

    def fill_s(held, o, to_ref, first=0, last=slots):
        for q in range(first, last):
            j, live = block(o, q)
            to_ref[q] = jnp.where(live, held[j // 8, j % 8], blank_wide)

    pairs = [pl.ds(2 * s, 2) for s in range(count)]
    copies_g = sends(send_g, land_g, gs_sem, gr_sem)
    copies_a = [sends(send_a, land_a, as_sem.at[s], ar_sem.at[s], pairs[s]) for s in range(count)]
    copies_b = sends(send_b, got_b, bs_sem, br_sem)
    passes_g = forwards(land_g, gfs_sem, gfr_sem)
    passes_a = [forwards(land_a, afs_sem.at[s], afr_sem.at[s], pairs[s]) for s in range(count)]
    passes_b = forwards(got_b, bfs_sem, bfr_sem)

    fetches[0].wait()
    def each_chip(fill):
        def one(o, _):
            fill(o)
            return 0
        lax.fori_loop(0, CHIPS, one, 0)

    def each_section(half):
        def one(r, _):
            pack((sec + r) % sections, half, xsend.at[half, r])
            return 0
        lax.fori_loop(1, sections, one, 0)

    each_chip(lambda o: fill_g(o, send_g.at[o]))
    land_g[me] = send_g[chip]
    for cp in fetches[1:]:
        cp.wait()
    each_section(0)
    pl.semaphore_wait(barrier, sections - 1 + 1 + len(chips))
    xcopies_a = xsends(0, xrecv_a)
    for cp in copies_g:
        cp.start()

    each_section(1)
    xcopies_b = xsends(1, xrecv_b)
    pack(sec, 0, xrecv_a.at[sec])
    pack(sec, 1, xrecv_b.at[sec])

    for cp in xcopies_a:
        cp.wait()
    for s in range(count):
        for o, cp in zip(chips + [chip], copies_a[s]):
            fill_s(xrecv_a, o, send_a.at[o], 2 * s, 2 * s + 2)
            cp.start()
    land_a[me] = send_a[chip]

    for cp in xcopies_b:
        cp.wait()
    each_chip(lambda o: fill_s(xrecv_b, o, send_b.at[o]))
    own_b = pltpu.make_async_copy(send_b.at[chip], got_b.at[me, every], out_sem.at[0])
    own_b.start()

    for cp, fw in zip(copies_g, passes_g):
        cp.wait_recv()
        fw.start()
    copies_g[-1].wait_recv()
    for fw in passes_g:
        fw.wait_recv()

    def flags(s):
        j, live = block(chip, 2 * s + core)
        return j % 4 < 2, live & (j % 2 == 0)

    for s in range(count):
        g = land_g[:, 2 * s + core].reshape(size)
        sums[s] = jnp.where(flags(s)[0], dotg(g, g, 1, 1), dotg(g, g, 0, 0))

    scale = (1.0 - ema_decay) / 512.0
    eye = (lax.broadcasted_iota(jnp.int32, size, 0) == lax.broadcasted_iota(jnp.int32, size, 1)).astype(f32)
    for s in range(count):
        for i, (cp, fw) in enumerate(zip(copies_a[s], passes_a[s])):
            cp.wait_recv()
            fw.start()
            if s == count - 1 and i == 9:
                for other in copies_b:
                    other.start()
        copies_a[s][-1].wait_recv()
        for fw in passes_a[s]:
            fw.wait_recv()
        q = 2 * s + core
        ema = split(ema_decay * whole_gram(land_a[:, q].reshape(512, WIDE)) + scale * sums[s])
        old = land_a[:, q, :, 384:].reshape(size)
        grown = dotg(ema[0], old, 1, 0) + dotg(ema[1], old, 1, 0)
        power[s] = grown
        ps = split(grown)
        cross[s] = jnp.where(flags(s)[1], dot3(ps, ps, 0, 0), eye)
    outs = [pltpu.make_async_copy(land_g, got_g.at[:, every], out_sem.at[1]),
            pltpu.make_async_copy(land_a, got_a.at[:, every], out_sem.at[2])]
    for cp in outs:
        cp.start()

    def share(p):
        part = pl.ds(0, count)
        return (pltpu.make_async_remote_copy(
            src_ref=fresh.at[p], dst_ref=got_f.at[core, p, part], send_sem=ffs_sem.at[p], recv_sem=ffr_sem.at[p],
            device_id=(sec, sibling), device_id_type=MESH),
            pltpu.make_async_copy(fresh.at[p], got_f.at[core, p, part], out_sem.at[3 + p]))

    def relay(p):
        for i in range(5 * p - 5, 5 * p):
            copies_b[i].wait_recv()
            passes_b[i].start()

    def step(p, _):
        factor_panel(p, cross, power, fresh, count)
        for cp in share(p):
            cp.start()
        for k in range(1, 4):
            pl.when(p == k)(functools.partial(relay, k))
        return 0
    lax.fori_loop(0, 4, step, 0)
    shared = [share(p)[0] for p in range(4)]
    outs += [share(p)[1] for p in range(4)]
    copies_b[-1].wait_recv()
    for cp in passes_b + shared:
        cp.wait_recv()
    own_b.wait()
    for cp in outs:
        cp.wait()
    for cp in copies_g + sum(copies_a, []) + copies_b + passes_g + sum(passes_a, []) + passes_b + shared:
        cp.wait_send()


def exchange(slots, moves, table, grad, lg, rg, lb, rb):
    smem = pl.BlockSpec(memory_space=pltpu.SMEM)
    anym = pl.BlockSpec(memory_space=pl.ANY)
    dma = pltpu.SemaphoreType.DMA
    count = slots // 2
    return pl.pallas_call(
        functools.partial(exchange_kernel, slots),
        out_shape=[
            jax.ShapeDtypeStruct((32, CHIP, 16, 512), bf16),
            jax.ShapeDtypeStruct((32, CHIP, 16, WIDE), bf16),
            jax.ShapeDtypeStruct((32, CHIP, 16, WIDE), bf16),
            jax.ShapeDtypeStruct((2, 4, CHIP // 2, 512, 128), bf16),
        ],
        in_specs=[smem] * 2 + [anym] * 5,
        out_specs=[anym] * 4,
        scratch_shapes=[
            pltpu.VMEM((32, 16, 512), bf16),
            pltpu.VMEM((4, 32, 16, 512), f32),
            pltpu.VMEM((2, 4, 8, 16, WIDE), bf16),
            pltpu.VMEM((4, 8, 16, WIDE), bf16),
            pltpu.VMEM((4, 8, 16, WIDE), bf16),
            pltpu.VMEM((CHIPS, slots, 16, 512), bf16),
            pltpu.VMEM((CHIPS, slots, 16, WIDE), bf16),
            pltpu.VMEM((CHIPS, slots, 16, WIDE), bf16),
            pltpu.VMEM((32, slots, 16, 512), bf16),
            pltpu.VMEM((32, slots, 16, WIDE), bf16),
            pltpu.VMEM((count, 512, 512), f32),
            pltpu.VMEM((count, 512, 512), f32),
            pltpu.VMEM((count, 512, 512), f32),
            pltpu.VMEM((4, count, 512, 128), bf16),
            dma((5,)), dma((2, 4)), dma((2, 4)),
            dma((16,)), dma((16,)), dma((count, 16)), dma((count, 16)), dma((16,)), dma((16,)),
            dma((15,)), dma((15,)), dma((count, 15)), dma((count, 15)), dma((15,)), dma((15,)),
            dma((4,)), dma((4,)), dma((7,)),
        ],
        compiler_params=pltpu.CompilerParams(
            collective_id=slots, has_side_effects=True, vmem_limit_bytes=40 << 20),
    )(moves, table, grad, lg, rg, lb, rb)


def finish_kernel(table_ref, got_g, got_a, got_b, got_f,
                  out_lg, out_rg, out_lb, out_rb, out_rot,
                  g_in, a_in, b_in, f_in, ema, basis, turned, in_sem, out_sem):
    size = (512, 512)
    scale = (1.0 - ema_decay) / 512.0

    def slot(c):
        word = table_ref[CHIPS * CHIP + c]
        q = word // 64
        loads = [pltpu.make_async_copy(got_g.at[:, q], g_in.at[c], in_sem.at[c, 0]),
                 pltpu.make_async_copy(got_a.at[:, q], a_in.at[c], in_sem.at[c, 1]),
                 pltpu.make_async_copy(got_b.at[:, q], b_in.at[c], in_sem.at[c, 2]),
                 pltpu.make_async_copy(got_f.at[q % 2, :, q // 2], f_in.at[c], in_sem.at[c, 3])]
        return word % 64 - 1, word > 0, loads

    def put(c, kind, src, mine, other, flag):
        @pl.when(flag)
        def _():
            pltpu.make_async_copy(src, mine.at[c], out_sem.at[c, kind]).start()

        @pl.when(jnp.logical_not(flag))
        def _():
            pltpu.make_async_copy(src, other.at[c], out_sem.at[c, kind]).start()

    for c in range(CAP):
        _, live, loads = slot(c)

        @pl.when(live)
        def _():
            for cp in loads:
                cp.start()

    for c in range(CAP):
        j, live, loads = slot(c)

        @pl.when(live)
        def _():
            for cp in loads:
                cp.wait()
            is_left = j % 4 < 2
            second = b_in[c, :, :, 384:].reshape(size)
            basis[c, 1] = second.astype(f32)
            put(c, 3, basis.at[c, 1], out_rb, out_lb, is_left)
            new = jnp.concatenate([f_in[c, p] for p in range(4)], axis=1)
            first = jnp.where(j % 2 == 0, new, a_in[c, :, :, 384:].reshape(size))
            basis[c, 0] = first.astype(f32)
            put(c, 2, basis.at[c, 0], out_lb, out_rb, is_left)
            g = g_in[c].reshape(size)
            outer = dotg(g, g, 1, 1)
            inner = dotg(g, g, 0, 0)
            ema[c, 0] = (ema_decay * whole_gram(a_in[c].reshape(512, WIDE))
                         + scale * jnp.where(is_left, outer, inner))
            put(c, 0, ema.at[c, 0], out_lg, out_rg, is_left)
            ema[c, 1] = (ema_decay * whole_gram(b_in[c].reshape(512, WIDE))
                         + scale * jnp.where(is_left, inner, outer))
            put(c, 1, ema.at[c, 1], out_rg, out_lg, is_left)
            low_left = jnp.where(is_left, first, second)
            low_right = jnp.where(is_left, second, first)
            half = dotg(low_left, g, 0, 0).astype(bf16)
            turned[c] = dotg(half, low_right, 1, 0).astype(bf16)
            pltpu.make_async_copy(turned.at[c], out_rot.at[c], out_sem.at[c, 4]).start()

        @pl.when(jnp.logical_not(live))
        def _():
            ema[c] = jnp.zeros((2,) + size, f32)
            turned[c] = jnp.zeros(size, bf16)
            for kind, out in enumerate((out_lg, out_rg, out_lb, out_rb)):
                pltpu.make_async_copy(ema.at[c, kind % 2], out.at[c], out_sem.at[c, kind]).start()
            pltpu.make_async_copy(turned.at[c], out_rot.at[c], out_sem.at[c, 4]).start()

    for c in range(CAP):
        for kind, out in enumerate((out_lg, out_rg, out_lb, out_rb)):
            pltpu.make_async_copy(ema.at[c, 0], out.at[c], out_sem.at[c, kind]).wait()
        pltpu.make_async_copy(turned.at[c], out_rot.at[c], out_sem.at[c, 4]).wait()


def finish(table, got_g, got_a, got_b, got_f):
    smem = pl.BlockSpec(memory_space=pltpu.SMEM)
    anym = pl.BlockSpec(memory_space=pl.ANY)
    full = jax.ShapeDtypeStruct((CAP, 512, 512), f32)
    return pl.pallas_call(
        finish_kernel,
        out_shape=[full] * 4 + [jax.ShapeDtypeStruct((CAP, 512, 512), bf16)],
        in_specs=[smem] + [anym] * 4,
        out_specs=[anym] * 5,
        scratch_shapes=[
            pltpu.VMEM((CAP, 32, 16, 512), bf16),
            pltpu.VMEM((CAP, 32, 16, WIDE), bf16),
            pltpu.VMEM((CAP, 32, 16, WIDE), bf16),
            pltpu.VMEM((CAP, 4, 512, 128), bf16),
            pltpu.VMEM((CAP, 2, 512, 512), f32),
            pltpu.VMEM((CAP, 2, 512, 512), f32),
            pltpu.VMEM((CAP, 512, 512), bf16),
            pltpu.SemaphoreType.DMA((CAP, 4)),
            pltpu.SemaphoreType.DMA((CAP, 5)),
        ],
        compiler_params=pltpu.CompilerParams(vmem_limit_bytes=28 << 20),
    )(table, got_g, got_a, got_b, got_f)


def shards(gradient, left_gram, right_gram, left_basis, right_basis, migration, owners):
    sections = lax.axis_size("section")
    blocks = gradient.shape[1]
    here_section = lax.axis_index("section")
    here_member = lax.axis_index("dp")
    listed = owners[:, :, 0]
    chip = lax.shift_right_logical(listed, 1)
    positions = jnp.arange(blocks, dtype=jnp.int32)
    before = positions[None, :] < positions[:, None]
    rank = jnp.sum(((listed[:, None, :] == listed[:, :, None]) & before).astype(jnp.int32), axis=2)
    chip_rank = jnp.sum(((chip[:, None, :] == chip[:, :, None]) & before).astype(jnp.int32), axis=2)
    few = jnp.max(chip_rank) < 4

    local = jnp.arange(sections, dtype=jnp.int32)[:, None] == here_section
    word = positions[None, :] + 1 + 64 * chip_rank
    place = jnp.where(local, chip * CHIP + chip_rank, -1)
    own = jnp.where(local & (listed == here_member), CHIPS * CHIP + rank, -1)
    entry = jnp.arange(CHIPS * CHIP + CAP, dtype=jnp.int32)[:, None, None]
    table = jnp.sum(jnp.where((place[None] == entry) | (own[None] == entry), word[None], 0), axis=(1, 2))

    got = lax.cond(few, functools.partial(exchange, 4), functools.partial(exchange, CHIP),
                   migration, table, gradient[0], left_gram[0], right_gram[0], left_basis[0], right_basis[0])
    outs = finish(table, *got)
    return tuple(o[None] for o in outs)


def solution(mesh):
    in_specs = (P("section", None, "dp", None),) * 5 + (P(), P())
    out_specs = (P("section", "dp", None, None),) * 5
    return jax.shard_map(shards, mesh=mesh, in_specs=in_specs, out_specs=out_specs, check_vma=False)
```
